512 devices in a mesh: block: 64 (over y_lo, z, core), view: 8 (over y_hi, x).
Axes of the slice: x: 4, y: 4 (y_hi: 2, y_lo: 2; y = y_hi * 2 + y_lo), z: 16, core: 2. Of those that a mesh axis runs over, the one named last changes fastest.
Arguments:
- estimate: float32 [64, 32, 48, 128], P('block'), may hold values from 0.5 to 2
- views_data: float32 [8, 64, 32, 48, 128], P('view', 'block'), may hold values from 0.1 to 10
- psf_taps: float32 [8, 3, 31], P('view'), may hold values from 0.05 to 1
- view_bounds: int32 [8, 4], replicated, may hold values from 0 to 512, as said below
Outputs:
- joined: float32 [64, 32, 48, 128], P('block')
The draws below stay inside these ranges and needn't reach their ends.
Inputs may be any that keep to these rules, and one draw needn't show every extreme that they name: `view_bounds`: for each view start < end along z and y, ends at most 512 along z and 192 along y; one view covers the whole grid.
All inputs are finite; a program needn't handle non-finite values.
Results may differ from the reference program's by a relative error of at most 0.0001.
Values sent between devices are 32-bit elements; how exact they have to be, the bound alone decides.
A program may use at most 192 MiB of HBM per device.

```python
import math
import jax
import jax.numpy as jnp
from jax import lax

Z_DEV = 32
Y_DEV = 48
X = 128
TAPS = 31
BY = 4
ITERS = 2
VIEWS = 8
NZ = 512
NY = 192
N_BLOCK = 64


def draw_view_bounds(key, part):
    key = jax.random.fold_in(key, 11)
    keys = jax.random.split(key, 5)
    z_start = jax.random.randint(keys[0], (VIEWS,), 0, NZ // 4 + 1)
    z_end = jax.random.randint(keys[1], (VIEWS,), NZ - NZ // 4, NZ + 1)
    y_start = jax.random.randint(keys[2], (VIEWS,), 0, NY // 4 + 1)
    y_end = jax.random.randint(keys[3], (VIEWS,), NY - NY // 4, NY + 1)
    chosen = jax.random.randint(keys[4], (), 0, VIEWS)
    whole = jnp.arange(VIEWS) == chosen
    z_start = jnp.where(whole, 0, z_start)
    z_end = jnp.where(whole, NZ, z_end)
    y_start = jnp.where(whole, 0, y_start)
    y_end = jnp.where(whole, NY, y_end)
    return jnp.stack([z_start, z_end, y_start, y_end], axis=1).astype(jnp.int32)


def block_levels(rng, shape, pieces, smallest, largest):
    def one(axis_at, shards_of):
        draws = jax.random.uniform(jax.random.fold_in(jax.random.fold_in(rng, 6), axis_at), (shards_of,), jnp.float32, smallest / len(pieces), largest / len(pieces))
        return jnp.repeat(jnp.exp(draws), shape[axis_at] // shards_of).reshape((-1,) + (1,) * (len(shape) - axis_at - 1))

    level = one(*pieces[0])
    for cut in pieces[1:]:
        level = level * one(*cut)
    return level


def setup_inputs(seed: int = 0) -> dict:
    splits = jax.random.split(jax.random.key(seed), 5)
    estimate = jnp.clip(jnp.exp(math.log(2.0) - 1.3862944 * jax.random.uniform(splits[0], (N_BLOCK, Z_DEV, Y_DEV, X), jnp.float32) ** block_levels(splits[0], (N_BLOCK, Z_DEV, Y_DEV, X), ((0, 64),), -0.2, 0.2)), 0.5, 2.0)
    views_data = jnp.clip(jnp.exp(math.log(10.0) - 4.6051702 * jax.random.uniform(splits[1], (VIEWS, N_BLOCK, Z_DEV, Y_DEV, X), jnp.float32) ** block_levels(splits[1], (VIEWS, N_BLOCK, Z_DEV, Y_DEV, X), ((0, 8), (1, 64)), -0.2, 0.2)), 0.1, 10.0)
    psf_taps = jnp.clip(jnp.exp(math.log(1.0) - 2.9957323 * jax.random.uniform(splits[2], (VIEWS, 3, TAPS), jnp.float32) ** block_levels(splits[2], (VIEWS, 3, TAPS), ((0, 8),), -0.2, 0.2)), 0.05, 1.0)
    view_bounds = draw_view_bounds(jax.random.fold_in(splits[4], 71), 0)
    return {"estimate": estimate, "views_data": views_data, "psf_taps": psf_taps, "view_bounds": view_bounds}


def assemble(blocks):
    rows = N_BLOCK // BY
    grid = blocks.reshape(rows, BY, Z_DEV, Y_DEV, X)
    return grid.transpose(0, 2, 1, 3, 4).reshape(rows * Z_DEV, BY * Y_DEV, X)


def split_blocks(volume):
    rows = N_BLOCK // BY
    grid = volume.reshape(rows, Z_DEV, BY, Y_DEV, X)
    return grid.transpose(0, 2, 1, 3, 4).reshape(N_BLOCK, Z_DEV, Y_DEV, X)


def correlate(field, taps, axis):
    half = TAPS // 2
    widths = [(0, 0), (0, 0), (0, 0)]
    widths[axis] = (half, half)
    padded = jnp.pad(field, widths)
    length = field.shape[axis]
    total = jnp.zeros_like(field)
    for tap in range(TAPS):
        piece = lax.slice_in_dim(padded, tap, tap + length, axis=axis)
        total = total + taps[tap] * piece
    return total


def blur(field, taps):
    field = correlate(field, taps[2], 2)
    field = correlate(field, taps[0], 0)
    return correlate(field, taps[1], 1)


def reference(estimate, views_data, psf_taps, view_bounds):
    volume = assemble(estimate)
    zpos = jnp.arange(NZ, dtype=jnp.int32)[:, None]
    ypos = jnp.arange(NY, dtype=jnp.int32)[None, :]
    masks = []
    for view in range(VIEWS):
        inside = (zpos >= view_bounds[view, 0]) & (zpos < view_bounds[view, 1])
        inside = inside & (ypos >= view_bounds[view, 2]) & (ypos < view_bounds[view, 3])
        masks.append(inside.astype(jnp.float32)[:, :, None])
    count = sum(masks)
    normed = psf_taps / jnp.sum(psf_taps, axis=2, keepdims=True)
    for step in range(ITERS):
        logs = jnp.zeros_like(volume)
        for view in range(VIEWS):
            taps = normed[view]
            blurred = blur(volume, taps)
            ratio = assemble(views_data[view]) / blurred
            correction = blur(ratio, taps[:, ::-1])
            logs = logs + masks[view] * jnp.log(correction)
        volume = volume * jnp.exp(logs / count)
    return split_blocks(volume)
```

```python
import functools

import jax
import jax.numpy as jnp
from jax import lax
from jax.experimental import pallas as pl
from jax.experimental.pallas import tpu as pltpu
from jax.sharding import PartitionSpec as P

MESH = pl.DeviceIdType.MESH
F32 = jnp.float32
BF16 = jnp.bfloat16

BY = 4
ITERS = 2
Z, Y, X = 32, 48, 128
TAPS = 31
HALF = 15
PAD = 16
VIEW_X, VIEW_Y = 4, 2
VIEWS = VIEW_X * VIEW_Y
PIECE = Z // VIEWS
YC = 16
NJ = Y // YC
ORDER = (0, 2, 1)
ZC = 8
NZC = Z // ZC


def split(x):
    hi = x.astype(BF16)
    lo = (x - hi.astype(F32)).astype(BF16)
    return hi, lo


def fill_tap(offset, taps, flip):
    acc = jnp.zeros(offset.shape, F32)
    for k in range(TAPS):
        at = TAPS - 1 - k if flip else k
        acc = jnp.where(offset == k, taps[:, at : at + 1], acc)
    return acc


def build_matrices(taps, kz_ref, ky_ref, wx_ref):
    tz, ty, tx = taps[0:1], taps[1:2], taps[2:3]
    for f in range(2):

        def z_rows(i, _):
            r0 = pl.multiple_of(i * 16, 16)
            row = lax.broadcasted_iota(jnp.int32, (16, 512), 0) + r0
            col = lax.broadcasted_iota(jnp.int32, (16, 512), 1)
            d = col - row
            k = jnp.where((d & 7) == 0, (d >> 3) - 1, -1)
            hi, lo = split(fill_tap(k, tz, f == 1))
            kz_ref[f, pl.ds(r0, 16), 0:512] = hi
            kz_ref[f, pl.ds(r0, 16), 512:1024] = hi
            kz_ref[f, pl.ds(r0, 16), 1024:1536] = lo
            return 0

        lax.fori_loop(0, 16, z_rows, 0)

        row = lax.broadcasted_iota(jnp.int32, (Y, 256), 0)
        col = lax.broadcasted_iota(jnp.int32, (Y, 256), 1)
        part = jnp.where(col >= 160, 2, jnp.where(col >= 80, 1, 0))
        k = jnp.where(col < 240, col - 80 * part - 1 - row, -1)
        val = fill_tap(k, ty, f == 1)
        hi = val.astype(BF16).astype(F32)
        ky_ref[f] = jnp.where(part == 2, val - hi, hi).astype(BF16)

        def x_rows(i, _):
            r0 = pl.multiple_of(i * 16, 16)
            row = lax.broadcasted_iota(jnp.int32, (16, 128), 0) + r0
            col = lax.broadcasted_iota(jnp.int32, (16, 128), 1)
            hi, lo = split(fill_tap(row - col + HALF, tx, f == 1))
            wx_ref[f, pl.ds(r0, 16), 0:128] = hi
            wx_ref[f, pl.ds(r0, 16), 128:256] = lo
            r1 = pl.multiple_of(r0 + 128, 16)
            wx_ref[f, pl.ds(r1, 16), 0:128] = hi
            wx_ref[f, pl.ds(r1, 16), 128:256] = jnp.zeros((16, 128), BF16)
            return 0

        lax.fori_loop(0, 8, x_rows, 0)


def z_blur(ext, kz):
    cols = [ext[:, 8 * g : 8 * g + 8, :].reshape(64 * 8, X) for g in range(YC // 8)]
    hi, lo = split(jnp.concatenate(cols, axis=1))
    stack = jnp.concatenate([hi, lo, hi], axis=0)
    return jnp.dot(kz, stack, preferred_element_type=F32)


def y_blur(planes, ky):
    hi, lo = split(jnp.concatenate(planes, axis=1))
    stack = jnp.concatenate([hi, lo, hi], axis=0)
    return jnp.dot(ky, stack, preferred_element_type=F32)


def x_blur(rows, wx):
    hi, lo = split(rows)
    out = jnp.dot(jnp.concatenate([hi, lo], axis=1), wx, preferred_element_type=F32)
    return out[:, :X] + out[:, X:]


def kernel(
    bounds_ref, taps_ref, est_ref, data_ref, out_ref,
    ef, ya, rb, eb, lg, rr, newf, dv, kz, ky, wx,
    lsem, zs, zr, ys, yr, rs_s, rs_r, ag_s, ag_r,
):
    b = lax.axis_index("block")
    v = lax.axis_index("view")
    vx, vy = lax.rem(v, VIEW_X), lax.div(v, VIEW_X)
    bz, by = lax.div(b, BY), lax.rem(b, BY)
    n_bz = lax.axis_size("block") // BY
    has_zlo, has_zhi = bz > 0, bz < n_bz - 1
    has_ylo, has_yhi = by > 0, by < BY - 1

    peers = []
    for dy in range(VIEW_Y):
        for dx in range(VIEW_X):
            if dx or dy:
                to = lax.rem(vy + dy, VIEW_Y) * VIEW_X + lax.rem(vx + dx, VIEW_X)
                frm = lax.rem(vy + VIEW_Y - dy, VIEW_Y) * VIEW_X + lax.rem(vx + VIEW_X - dx, VIEW_X)
                peers.append((to, frm))

    load_est = pltpu.make_async_copy(est_ref.at[0], ef.at[0, pl.ds(PAD, Z)], lsem.at[0])
    load_data = pltpu.make_async_copy(data_ref.at[0, 0], dv, lsem.at[1])
    load_est.start()
    load_data.start()

    bar = pltpu.get_barrier_semaphore()
    total = jnp.int32(VIEWS - 1)
    for cond, dst in ((has_zlo, b - BY), (has_zhi, b + BY), (has_ylo, b - 1), (has_yhi, b + 1)):
        total = total + cond.astype(jnp.int32)

        @pl.when(cond)
        def _():
            pl.semaphore_signal(bar, inc=1, device_id={"block": dst}, device_id_type=MESH)

    for to, _ in peers:
        pl.semaphore_signal(bar, inc=1, device_id={"view": to}, device_id_type=MESH)

    for it in range(ITERS):
        for buf in (ef, eb):
            buf[it, 0] = jnp.zeros((Y, X), F32)
            buf[it, 63] = jnp.zeros((Y, X), F32)

            @pl.when(jnp.logical_not(has_zlo))
            def _():
                buf[it, 1:PAD] = jnp.zeros((HALF, Y, X), F32)

            @pl.when(jnp.logical_not(has_zhi))
            def _():
                buf[it, PAD + Z : PAD + Z + HALF] = jnp.zeros((HALF, Y, X), F32)

        for buf in (ya, rb):

            @pl.when(jnp.logical_not(has_ylo))
            def _():
                buf[it, :, 0:PAD, :] = jnp.zeros((Z, PAD, X), F32)

            @pl.when(jnp.logical_not(has_yhi))
            def _():
                buf[it, :, PAD + Y :, :] = jnp.zeros((Z, PAD, X), F32)

    load_est.wait()
    load_data.wait()
    pl.semaphore_wait(bar, total)

    def z_copies(buf, it, which, j):
        rows = pl.ds(YC * j, YC)
        up = pltpu.make_async_remote_copy(
            src_ref=buf.at[it, pl.ds(PAD + Z - HALF, HALF), rows],
            dst_ref=buf.at[it, pl.ds(1, HALF), rows],
            send_sem=zs.at[it, which, 0, j], recv_sem=zr.at[it, which, 0, j],
            device_id={"block": b + BY}, device_id_type=MESH)
        down = pltpu.make_async_remote_copy(
            src_ref=buf.at[it, pl.ds(PAD, HALF), rows],
            dst_ref=buf.at[it, pl.ds(PAD + Z, HALF), rows],
            send_sem=zs.at[it, which, 1, j], recv_sem=zr.at[it, which, 1, j],
            device_id={"block": b - BY}, device_id_type=MESH)
        return up, down

    def y_copies(buf, it, which, c):
        planes = pl.ds(ZC * c, ZC)
        up = pltpu.make_async_remote_copy(
            src_ref=buf.at[it, planes, pl.ds(Y, PAD)],
            dst_ref=buf.at[it, planes, pl.ds(0, PAD)],
            send_sem=ys.at[it, which, 0, c], recv_sem=yr.at[it, which, 0, c],
            device_id={"block": b + 1}, device_id_type=MESH)
        down = pltpu.make_async_remote_copy(
            src_ref=buf.at[it, planes, pl.ds(PAD, PAD)],
            dst_ref=buf.at[it, planes, pl.ds(PAD + Y, PAD)],
            send_sem=ys.at[it, which, 1, c], recv_sem=yr.at[it, which, 1, c],
            device_id={"block": b - 1}, device_id_type=MESH)
        return up, down

    def start(pair, lo, hi):
        up, down = pair

        @pl.when(hi)
        def _():
            up.start()

        @pl.when(lo)
        def _():
            down.start()

    def wait_recv(pair, lo, hi):
        up, down = pair

        @pl.when(lo)
        def _():
            up.wait_recv()

        @pl.when(hi)
        def _():
            down.wait_recv()

    def wait_send(pair, lo, hi):
        up, down = pair

        @pl.when(hi)
        def _():
            up.wait_send()

        @pl.when(lo)
        def _():
            down.wait_send()

    zsent, ysent, vsent = [], [], []

    def send_z(buf, it, which, j):
        pair = z_copies(buf, it, which, j)
        start(pair, has_zlo, has_zhi)
        zsent.append(pair)

    def send_y(buf, it, which, c):
        pair = y_copies(buf, it, which, c)
        start(pair, has_ylo, has_yhi)
        ysent.append(pair)

    for j in ORDER:
        send_z(ef, 0, 0, j)

    taps = taps_ref[0]
    taps = taps / jnp.sum(taps, axis=1, keepdims=True)
    build_matrices(taps, kz, ky, wx)

    z0, y0 = bz * Z, by * Y
    ypos = lax.broadcasted_iota(jnp.int32, (Y, X), 0) + y0
    own_y = jnp.where((ypos >= bounds_ref[v, 2]) & (ypos < bounds_ref[v, 3]), 1.0, 0.0).astype(F32)

    def own_z(plane):
        zpos = z0 + plane
        return (zpos >= bounds_ref[v, 0]) & (zpos < bounds_ref[v, 1])

    for it in range(ITERS):
        for j in ORDER:
            wait_recv(z_copies(ef, it, 0, j), has_zlo, has_zhi)
            res = z_blur(ef[it, :, YC * j : YC * (j + 1), :], kz[0])
            for g in range(YC // 8):
                r0 = PAD + YC * j + 8 * g
                ya[it, :, r0 : r0 + 8, :] = res[:, X * g : X * (g + 1)].reshape(Z, 8, X)
        for c in range(NZC):
            send_y(ya, it, 0, c)
        for c in range(NZC):
            wait_recv(y_copies(ya, it, 0, c), has_ylo, has_yhi)
            parts = []
            for p in range(ZC * c, ZC * (c + 1), 2):
                res = y_blur([ya[it, p], ya[it, p + 1]], ky[0][:, :240])
                parts += [res[:, :X], res[:, X:]]
            blurred = x_blur(jnp.concatenate(parts, axis=0), wx[0])
            ratio = dv[ZC * c : ZC * (c + 1)].reshape(ZC * Y, X) / blurred
            rb[it, ZC * c : ZC * (c + 1), PAD : PAD + Y, :] = x_blur(ratio, wx[1]).reshape(ZC, Y, X)
            send_y(rb, it, 1, c)
        for c in range(NZC):
            wait_recv(y_copies(rb, it, 1, c), has_ylo, has_yhi)
            for p in range(ZC * c, ZC * (c + 1), 2):
                res = y_blur([rb[it, p], rb[it, p + 1]], ky[1][:, :240])
                eb[it, PAD + p] = res[:, :X]
                eb[it, PAD + p + 1] = res[:, X:]
        for j in ORDER:
            send_z(eb, it, 1, j)
        for j in ORDER:
            wait_recv(z_copies(eb, it, 1, j), has_zlo, has_zhi)
            res = z_blur(eb[it, :, YC * j : YC * (j + 1), :], kz[1])
            for g in range(YC // 8):
                r0 = YC * j + 8 * g
                logs = jnp.log(res[:, X * g : X * (g + 1)].reshape(Z, 8, X))
                for p in range(Z):
                    keep = jnp.where(own_z(p), own_y[r0 : r0 + 8], 0.0)
                    lg[it, p, r0 : r0 + 8, :] = keep * logs[p]
            rows = pl.ds(YC * j, YC)
            for i, (to, frm) in enumerate(peers):
                cp = pltpu.make_async_remote_copy(
                    src_ref=lg.at[it, pl.ds(to * PIECE, PIECE), rows],
                    dst_ref=rr.at[it, i, :, rows],
                    send_sem=rs_s.at[it, i, j], recv_sem=rs_r.at[it, i, j],
                    device_id={"view": to}, device_id_type=MESH)
                cp.start()
                vsent.append(cp)
        mine = v * PIECE
        for j in ORDER:
            rows = pl.ds(YC * j, YC)
            acc = lg[it, pl.ds(mine, PIECE), YC * j : YC * (j + 1), :]
            for i in range(VIEWS - 1):
                pltpu.make_async_remote_copy(
                    src_ref=lg.at[it, pl.ds(0, PIECE), rows], dst_ref=rr.at[it, i, :, rows],
                    send_sem=rs_s.at[it, i, j], recv_sem=rs_r.at[it, i, j],
                    device_id={"view": peers[i][0]}, device_id_type=MESH).wait_recv()
                acc = acc + rr[it, i, :, YC * j : YC * (j + 1), :]
            yj = ypos[YC * j : YC * (j + 1)]
            ins = [
                jnp.where((yj >= bounds_ref[w, 2]) & (yj < bounds_ref[w, 3]), 1.0, 0.0).astype(F32)
                for w in range(VIEWS)
            ]
            for p in range(PIECE):
                zpos = z0 + mine + p
                count = jnp.zeros((YC, X), F32)
                for w in range(VIEWS):
                    inz = (zpos >= bounds_ref[w, 0]) & (zpos < bounds_ref[w, 1])
                    count = count + jnp.where(inz, ins[w], 0.0)
                old = ef[it, PAD + mine + p, YC * j : YC * (j + 1), :]
                new = old * jnp.exp(acc[p] / count)
                newf[it, p, YC * j : YC * (j + 1), :] = new
                if it < ITERS - 1:
                    ef[it + 1, PAD + mine + p, YC * j : YC * (j + 1), :] = new
            if it < ITERS - 1:
                target = ef.at[it + 1, pl.ds(PAD + mine, PIECE), rows]
            else:
                target = out_ref.at[0, pl.ds(mine, PIECE), rows]
                cp = pltpu.make_async_copy(newf.at[it, :, rows], target, lsem.at[2 + j])
                cp.start()
                vsent.append(cp)
            for i, (to, frm) in enumerate(peers):
                cp = pltpu.make_async_remote_copy(
                    src_ref=newf.at[it, :, rows], dst_ref=target,
                    send_sem=ag_s.at[it, i, j], recv_sem=ag_r.at[it, i, j],
                    device_id={"view": to}, device_id_type=MESH)
                cp.start()
                vsent.append(cp)
        for j in ORDER:
            rows = pl.ds(YC * j, YC)
            for i, (to, frm) in enumerate(peers):
                if it < ITERS - 1:
                    target = ef.at[it + 1, pl.ds(PAD + frm * PIECE, PIECE), rows]
                else:
                    target = out_ref.at[0, pl.ds(frm * PIECE, PIECE), rows]
                pltpu.make_async_remote_copy(
                    src_ref=newf.at[it, :, rows], dst_ref=target,
                    send_sem=ag_s.at[it, i, j], recv_sem=ag_r.at[it, i, j],
                    device_id={"view": to}, device_id_type=MESH).wait_recv()
            if it < ITERS - 1:
                send_z(ef, it + 1, 0, j)

    for pair in zsent:
        wait_send(pair, has_zlo, has_zhi)
    for pair in ysent:
        wait_send(pair, has_ylo, has_yhi)
    for cp in vsent:
        if cp.is_remote:
            cp.wait_send()
        else:
            cp.wait()


def body(estimate, views_data, psf_taps, view_bounds):
    dma = pltpu.SemaphoreType.DMA
    return pl.pallas_call(
        kernel,
        out_shape=jax.ShapeDtypeStruct(estimate.shape, F32),
        in_specs=[
            pl.BlockSpec(memory_space=pltpu.SMEM),
            pl.BlockSpec(memory_space=pltpu.VMEM),
            pl.BlockSpec(memory_space=pl.ANY),
            pl.BlockSpec(memory_space=pl.ANY),
        ],
        out_specs=pl.BlockSpec(memory_space=pl.ANY),
        scratch_shapes=[
            pltpu.VMEM((ITERS, 64, Y, X), F32),
            pltpu.VMEM((ITERS, Z, 80, X), F32),
            pltpu.VMEM((ITERS, Z, 80, X), F32),
            pltpu.VMEM((ITERS, 64, Y, X), F32),
            pltpu.VMEM((ITERS, Z, Y, X), F32),
            pltpu.VMEM((ITERS, VIEWS - 1, PIECE, Y, X), F32),
            pltpu.VMEM((ITERS, PIECE, Y, X), F32),
            pltpu.VMEM((Z, Y, X), F32),
            pltpu.VMEM((2, 256, 1536), BF16),
            pltpu.VMEM((2, Y, 256), BF16),
            pltpu.VMEM((2, 256, 256), BF16),
            dma((2 + NJ,)),
            dma((ITERS, 2, 2, NJ)),
            dma((ITERS, 2, 2, NJ)),
            dma((ITERS, 2, 2, NZC)),
            dma((ITERS, 2, 2, NZC)),
            dma((ITERS, VIEWS - 1, NJ)),
            dma((ITERS, VIEWS - 1, NJ)),
            dma((ITERS, VIEWS - 1, NJ)),
            dma((ITERS, VIEWS - 1, NJ)),
        ],
        compiler_params=pltpu.CompilerParams(
            collective_id=0, has_side_effects=True, vmem_limit_bytes=48 << 20
        ),
        name="deconvolve",
    )(view_bounds, psf_taps, estimate, views_data)


def solution(mesh):
    return jax.shard_map(
        body,
        mesh=mesh,
        in_specs=(
            P("block", None, None, None),
            P("view", "block", None, None, None),
            P("view", None, None),
            P(),
        ),
        out_specs=P("block", None, None, None),
        check_vma=False,
    )
```

```python
import functools

import jax
import jax.numpy as jnp
from jax import lax
from jax.experimental import pallas as pl
from jax.experimental.pallas import tpu as pltpu
from jax.sharding import PartitionSpec as P

MESH = pl.DeviceIdType.MESH
F32 = jnp.float32
BF16 = jnp.bfloat16

BY = 4
ITERS = 2
Z, Y, X = 32, 48, 128
TAPS = 31
HALF = 15
PAD = 16
VIEW_X, VIEW_Y = 4, 2
VIEWS = VIEW_X * VIEW_Y
PIECE = Z // VIEWS
YC = 8
NJ = Y // YC
ORDER = (2, 3, 0, 1, 4, 5)
FIRST_YC = 16
FIRST_NJ = Y // FIRST_YC
FIRST = (0, 2, 1)
DIRECT = HALF - VIEWS
ZC = 8
NZC = Z // ZC


def split(x):
    hi = x.astype(BF16)
    lo = (x - hi.astype(F32)).astype(BF16)
    return hi, lo


def fill_tap(offset, taps, flip):
    acc = jnp.zeros(offset.shape, F32)
    for k in range(TAPS):
        at = TAPS - 1 - k if flip else k
        acc = jnp.where(offset == k, taps[:, at : at + 1], acc)
    return acc


def build_z(taps, kz_ref, f):
    def z_rows(i, _):
        r0 = pl.multiple_of(i * 16, 16)
        row = lax.broadcasted_iota(jnp.int32, (16, 512), 0) + r0
        col = lax.broadcasted_iota(jnp.int32, (16, 512), 1)
        k = jnp.where((col & 7) == (row & 7), (col >> 3) - 1 - (row >> 3), -1)
        hi, lo = split(fill_tap(k, taps[0], f == 1))
        kz_ref[f, pl.ds(r0, 16), 0:512] = hi
        kz_ref[f, pl.ds(r0, 16), 512:1024] = hi
        kz_ref[f, pl.ds(r0, 16), 1024:1536] = lo
        return 0

    lax.fori_loop(0, 16, z_rows, 0)


def build_xy(taps, ko_ref, kr_ref, wx_ref, f):
    row = lax.broadcasted_iota(jnp.int32, (Y, 256), 0)
    col = lax.broadcasted_iota(jnp.int32, (Y, 256), 1)
    part = jnp.where(col >= 96, 2, jnp.where(col >= 48, 1, 0))
    k = jnp.where(col < 144, col - 48 * part - row + HALF, -1)
    val = fill_tap(k, taps[1], f == 1)
    hi = val.astype(BF16).astype(F32)
    ko_ref[f] = jnp.where(part == 2, val - hi, hi).astype(BF16)

    row = lax.broadcasted_iota(jnp.int32, (2 * PAD, 128), 0)
    col = lax.broadcasted_iota(jnp.int32, (2 * PAD, 128), 1)
    part = jnp.where(col >= 64, 2, jnp.where(col >= 32, 1, 0))
    at = col - 32 * part
    source = jnp.where(at < PAD, at - PAD, at + Y - PAD)
    target = jnp.where(row < PAD, row, row + Y - 2 * PAD)
    k = jnp.where(col < 96, source - target + HALF, -1)
    val = fill_tap(k, taps[1], f == 1)
    hi = val.astype(BF16).astype(F32)
    kr_ref[f] = jnp.where(part == 2, val - hi, hi).astype(BF16)

    def x_rows(i, _):
        r0 = pl.multiple_of(i * 16, 16)
        row = lax.broadcasted_iota(jnp.int32, (16, 128), 0) + r0
        col = lax.broadcasted_iota(jnp.int32, (16, 128), 1)
        hi, lo = split(fill_tap(row - col + HALF, taps[2], f == 1))
        wx_ref[f, pl.ds(r0, 16), 0:128] = hi
        wx_ref[f, pl.ds(r0, 16), 128:256] = lo
        r1 = pl.multiple_of(r0 + 128, 16)
        wx_ref[f, pl.ds(r1, 16), 0:128] = hi
        wx_ref[f, pl.ds(r1, 16), 128:256] = jnp.zeros((16, 128), BF16)
        return 0

    lax.fori_loop(0, 8, x_rows, 0)


def z_blur(ext, kz):
    cols = [ext[:, 8 * g : 8 * g + 8, :].reshape(64 * 8, X) for g in range(ext.shape[1] // 8)]
    hi, lo = split(jnp.concatenate(cols, axis=1))
    stack = jnp.concatenate([hi, lo, hi], axis=0)
    return jnp.dot(kz, stack, preferred_element_type=F32)


def y_blur(planes, ky):
    hi, lo = split(jnp.concatenate(planes, axis=1))
    stack = jnp.concatenate([hi, lo, hi], axis=0)
    return jnp.dot(ky, stack, preferred_element_type=F32)


def x_blur(rows, wx):
    hi, lo = split(rows)
    out = jnp.dot(jnp.concatenate([hi, lo], axis=1), wx, preferred_element_type=F32)
    return out[:, :X] + out[:, X:]


def kernel(
    bounds_ref, taps_ref, est_ref, data_ref, out_ref,
    ef, ya, rb, eb, lg, rr, newf, dv, pa, taps_v, kz, ko, kr, wx,
    lsem, zs, zr, hs, hr, fs, fr, ys, yr, rs_s, rs_r, ag_s, ag_r,
):
    b = lax.axis_index("block")
    v = lax.axis_index("view")
    vx, vy = lax.rem(v, VIEW_X), lax.div(v, VIEW_X)
    bz, by = lax.div(b, BY), lax.rem(b, BY)
    n_bz = lax.axis_size("block") // BY
    has_zlo, has_zhi = bz > 0, bz < n_bz - 1
    has_ylo, has_yhi = by > 0, by < BY - 1

    peers = []
    for dy in range(VIEW_Y):
        for dx in range(VIEW_X):
            if dx or dy:
                to = lax.rem(vy + dy, VIEW_Y) * VIEW_X + lax.rem(vx + dx, VIEW_X)
                frm = lax.rem(vy + VIEW_Y - dy, VIEW_Y) * VIEW_X + lax.rem(vx + VIEW_X - dx, VIEW_X)
                peers.append((to, frm))

    load_est = pltpu.make_async_copy(est_ref.at[0], ef.at[0, pl.ds(PAD, Z)], lsem.at[0])
    load_data = pltpu.make_async_copy(data_ref.at[0, 0], dv, lsem.at[1])
    load_taps = pltpu.make_async_copy(taps_ref, taps_v, lsem.at[2])
    load_est.start()
    load_data.start()
    load_taps.start()

    bar = pltpu.get_barrier_semaphore()
    total = jnp.int32(VIEWS - 1)
    for cond, dst in ((has_zlo, b - BY), (has_zhi, b + BY), (has_ylo, b - 1), (has_yhi, b + 1)):
        total = total + cond.astype(jnp.int32)

        @pl.when(cond)
        def _():
            pl.semaphore_signal(bar, inc=1, device_id={"block": dst}, device_id_type=MESH)

    for to, _ in peers:
        pl.semaphore_signal(bar, inc=1, device_id={"view": to}, device_id_type=MESH)

    for it in range(ITERS):
        for buf in (ef, eb):
            buf[it, 0] = jnp.zeros((Y, X), F32)
            buf[it, 63] = jnp.zeros((Y, X), F32)

        @pl.when(jnp.logical_not(has_zlo))
        def _():
            eb[it, 1:PAD] = jnp.zeros((HALF, Y, X), F32)

        @pl.when(jnp.logical_not(has_zhi))
        def _():
            eb[it, PAD + Z : PAD + Z + HALF] = jnp.zeros((HALF, Y, X), F32)

        low = pl.ds(1, HALF) if it else pl.ds(1 + VIEWS, DIRECT)
        high = pl.ds(PAD + Z, HALF if it else DIRECT)

        @pl.when(jnp.logical_not(has_zlo))
        def _():
            if it == 0:
                ef[it, 1 + v] = jnp.zeros((Y, X), F32)
            ef[it, low] = jnp.zeros((low.size, Y, X), F32)

        @pl.when(jnp.logical_not(has_zhi))
        def _():
            if it == 0:
                ef[it, PAD + Z + DIRECT + v] = jnp.zeros((Y, X), F32)
            ef[it, high] = jnp.zeros((high.size, Y, X), F32)

        for buf in (ya, rb):

            @pl.when(jnp.logical_not(has_ylo))
            def _():
                buf[it, :, 0:PAD, :] = jnp.zeros((Z, PAD, X), F32)

            @pl.when(jnp.logical_not(has_yhi))
            def _():
                buf[it, :, PAD + Y :, :] = jnp.zeros((Z, PAD, X), F32)

    load_est.wait()
    pl.semaphore_wait(bar, total)

    def pair_of(buf, it, up, down, count, rows, sems, recvs, key, step):
        one = pltpu.make_async_remote_copy(
            src_ref=buf.at[it, pl.ds(up[0], count), rows], dst_ref=buf.at[it, pl.ds(up[1], count), rows],
            send_sem=sems.at[(it, 0) + key], recv_sem=recvs.at[(it, 0) + key],
            device_id={"block": b + step}, device_id_type=MESH)
        two = pltpu.make_async_remote_copy(
            src_ref=buf.at[it, pl.ds(down[0], count), rows], dst_ref=buf.at[it, pl.ds(down[1], count), rows],
            send_sem=sems.at[(it, 1) + key], recv_sem=recvs.at[(it, 1) + key],
            device_id={"block": b - step}, device_id_type=MESH)
        return one, two

    def ratio_rims(it, j):
        rows = pl.ds(YC * j, YC)
        return pair_of(eb, it, (PAD + Z - HALF, 1), (PAD, PAD + Z), HALF, rows, zs, zr, (1, j), BY)

    def estimate_rims(it, j):
        rows = pl.ds(YC * j, YC)
        return pair_of(ef, it, (PAD + Z - HALF, 1), (PAD, PAD + Z), HALF, rows, zs, zr, (0, j), BY)

    def direct_rims(j):
        rows = pl.ds(FIRST_YC * j, FIRST_YC)
        return pair_of(ef, 0, (PAD + Z - DIRECT, 1 + VIEWS), (PAD, PAD + Z), DIRECT, rows, zs, zr, (0, j), BY)

    def shared_rims(j):
        rows = pl.ds(FIRST_YC * j, FIRST_YC)
        return pair_of(ef, 0, (PAD + 17 + v, 1 + v), (PAD + DIRECT + v, PAD + Z + DIRECT + v), 1, rows, hs, hr, (j,), BY)

    def forwards(j, w):
        rows = pl.ds(FIRST_YC * j, FIRST_YC)
        out = []
        for i, (to, frm) in enumerate(peers):
            for h, first in enumerate((1, PAD + Z + DIRECT)):
                plane = pl.ds(first + (v if w else frm), 1)
                out.append(pltpu.make_async_remote_copy(
                    src_ref=ef.at[0, plane, rows], dst_ref=ef.at[0, plane, rows],
                    send_sem=fs.at[h, i, j], recv_sem=fr.at[h, i, j],
                    device_id={"view": to}, device_id_type=MESH))
        return out

    def y_pair(buf, it, which, planes, n, c, half):
        up = pltpu.make_async_remote_copy(
            src_ref=buf.at[it, planes, pl.ds(Y + half, n)], dst_ref=buf.at[it, planes, pl.ds(half, n)],
            send_sem=ys.at[it, which, 0, c], recv_sem=yr.at[it, which, 0, c],
            device_id={"block": b + 1}, device_id_type=MESH)
        down = pltpu.make_async_remote_copy(
            src_ref=buf.at[it, planes, pl.ds(PAD + half, n)], dst_ref=buf.at[it, planes, pl.ds(PAD + Y + half, n)],
            send_sem=ys.at[it, which, 1, c], recv_sem=yr.at[it, which, 1, c],
            device_id={"block": b - 1}, device_id_type=MESH)
        return up, down

    def blurred_rims(it, h):
        return y_pair(ya, it, 0, pl.ds(0, Z), 8, h, 8 * h)

    def ratio_y_rims(it, c):
        return y_pair(rb, it, 1, pl.ds(ZC * c, ZC), PAD, c, 0)

    def start(pair, lo, hi):
        up, down = pair

        @pl.when(hi)
        def _():
            up.start()

        @pl.when(lo)
        def _():
            down.start()

    def wait_recv(pair, lo, hi):
        up, down = pair

        @pl.when(lo)
        def _():
            up.wait_recv()

        @pl.when(hi)
        def _():
            down.wait_recv()

    def wait_send(pair, lo, hi):
        up, down = pair

        @pl.when(hi)
        def _():
            up.wait_send()

        @pl.when(lo)
        def _():
            down.wait_send()

    zsent, ysent, vsent = [], [], []

    def send_z(pair):
        start(pair, has_zlo, has_zhi)
        zsent.append(pair)

    def send_y(up, down):
        if up is not None:

            @pl.when(has_yhi)
            def _():
                up.start()

            ysent.append((has_yhi, up))
        if down is not None:

            @pl.when(has_ylo)
            def _():
                down.start()

            ysent.append((has_ylo, down))

    def start_up(pair):
        @pl.when(has_zhi)
        def _():
            pair[0].start()

    def start_down(pair):
        @pl.when(has_zlo)
        def _():
            pair[1].start()

    for j in FIRST:
        send_z(shared_rims(j))
    for j in FIRST:
        send_z(direct_rims(j))

    load_taps.wait()
    taps = taps_v[...]
    taps = taps / jnp.sum(taps, axis=2, keepdims=True)
    build_z(taps, kz, 0)

    z0, y0 = bz * Z, by * Y
    ypos = lax.broadcasted_iota(jnp.int32, (Y, X), 0) + y0
    own_y = jnp.where((ypos >= bounds_ref[2, v]) & (ypos < bounds_ref[3, v]), 1.0, 0.0).astype(F32)

    def own_z(plane):
        zpos = z0 + plane
        return (zpos >= bounds_ref[0, v]) & (zpos < bounds_ref[1, v])

    def blur_rows(it, r0, rows):
        res = z_blur(ef[it, :, r0 : r0 + rows, :], kz[0])
        for r in range(r0, r0 + rows, 8):
            at = X * ((r - r0) // 8)
            ya[it, :, PAD + r : PAD + r + 8, :] = res[:, at : at + X].reshape(Z, 8, X)
            if r < PAD:
                send_y(None, blurred_rims(it, r // 8)[1])
            if r >= Y - PAD:
                send_y(blurred_rims(it, (r - Y + PAD) // 8)[0], None)

    for j in FIRST:
        wait_recv(shared_rims(j), has_zlo, has_zhi)
        for cp in forwards(j, True):
            cp.start()
            vsent.append(cp)
    build_xy(taps, ko, kr, wx, 0)
    build_xy(taps, ko, kr, wx, 1)
    build_z(taps, kz, 1)
    load_data.wait()
    for j in FIRST:
        wait_recv(direct_rims(j), has_zlo, has_zhi)
        for cp in forwards(j, False):
            cp.wait_recv()
        blur_rows(0, FIRST_YC * j, FIRST_YC)

    for it in range(ITERS):
        own = slice(PAD, PAD + Y)
        for p in range(0, Z, 2):
            res = y_blur([ya[it, p, own], ya[it, p + 1, own]], ko[0][:, :144])
            pa[p] = res[:, :X]
            pa[p + 1] = res[:, X:]
        for h in range(2):
            wait_recv(blurred_rims(it, h), has_ylo, has_yhi)

        def rims(buf, p):
            return jnp.concatenate([buf[it, p, 0:PAD], buf[it, p, PAD + Y :]], axis=0)

        for c in range(NZC):
            span = range(ZC * c, ZC * (c + 1), 2)
            parts = []
            for p in span:
                res = y_blur([rims(ya, p), rims(ya, p + 1)], kr[0][:, :96])
                for h in range(2):
                    edge = res[:, X * h : X * (h + 1)]
                    parts += [pa[p + h, 0:PAD] + edge[:PAD], pa[p + h, PAD : 2 * PAD], pa[p + h, 2 * PAD :] + edge[PAD:]]
            blurred = x_blur(jnp.concatenate(parts, axis=0), wx[0])
            ratio = dv[ZC * c : ZC * (c + 1)].reshape(ZC * Y, X) / blurred
            rb[it, ZC * c : ZC * (c + 1), own, :] = x_blur(ratio, wx[1]).reshape(ZC, Y, X)
            send_y(*ratio_y_rims(it, c))
            for p in span:
                res = y_blur([rb[it, p, own], rb[it, p + 1, own]], ko[1][:, :144])
                eb[it, PAD + p] = res[:, :X]
                eb[it, PAD + p + 1] = res[:, X:]
            if c == NZC // 2 - 1:
                for j in ORDER[:2]:
                    pair = ratio_rims(it, j)
                    zsent.append(pair)
                    start_down(pair)
        for j in ORDER[:2]:
            start_up(ratio_rims(it, j))
        for c in range(NZC):
            wait_recv(ratio_y_rims(it, c), has_ylo, has_yhi)
            for p in range(ZC * c, ZC * (c + 1), 2):
                res = y_blur([rims(rb, p), rims(rb, p + 1)], kr[1][:, :96])
                for h in range(2):
                    edge = res[:, X * h : X * (h + 1)]
                    eb[it, PAD + p + h, 0:PAD] += edge[:PAD]
                    eb[it, PAD + p + h, 2 * PAD :] += edge[PAD:]
            if c == NZC // 2 - 1:
                for j in ORDER[2:]:
                    pair = ratio_rims(it, j)
                    zsent.append(pair)
                    start_down(pair)
        for j in ORDER[2:]:
            start_up(ratio_rims(it, j))

        mine = v * PIECE

        def log_step(j):
            wait_recv(ratio_rims(it, j), has_zlo, has_zhi)
            res = z_blur(eb[it, :, YC * j : YC * (j + 1), :], kz[1])
            for g in range(YC // 8):
                r0 = YC * j + 8 * g
                logs = jnp.log(res[:, X * g : X * (g + 1)].reshape(Z, 8, X))
                for p in range(Z):
                    keep = jnp.where(own_z(p), own_y[r0 : r0 + 8], 0.0)
                    lg[it, p, r0 : r0 + 8, :] = keep * logs[p]
            rows = pl.ds(YC * j, YC)
            for i, (to, frm) in enumerate(peers):
                cp = pltpu.make_async_remote_copy(
                    src_ref=lg.at[it, pl.ds(to * PIECE, PIECE), rows],
                    dst_ref=rr.at[it, i, :, rows],
                    send_sem=rs_s.at[it, i, j], recv_sem=rs_r.at[it, i, j],
                    device_id={"view": to}, device_id_type=MESH)
                cp.start()
                vsent.append(cp)

        def sum_step(j):
            rows = pl.ds(YC * j, YC)
            acc = lg[it, pl.ds(mine, PIECE), YC * j : YC * (j + 1), :]
            for i in range(VIEWS - 1):
                pltpu.make_async_remote_copy(
                    src_ref=lg.at[it, pl.ds(0, PIECE), rows], dst_ref=rr.at[it, i, :, rows],
                    send_sem=rs_s.at[it, i, j], recv_sem=rs_r.at[it, i, j],
                    device_id={"view": peers[i][0]}, device_id_type=MESH).wait_recv()
                acc = acc + rr[it, i, :, YC * j : YC * (j + 1), :]
            yj = ypos[YC * j : YC * (j + 1)]
            ins = [
                jnp.where((yj >= bounds_ref[2, w]) & (yj < bounds_ref[3, w]), 1.0, 0.0).astype(F32)
                for w in range(VIEWS)
            ]
            for p in range(PIECE):
                zpos = z0 + mine + p
                count = jnp.zeros((YC, X), F32)
                for w in range(VIEWS):
                    inz = (zpos >= bounds_ref[0, w]) & (zpos < bounds_ref[1, w])
                    count = count + jnp.where(inz, ins[w], 0.0)
                old = ef[it, PAD + mine + p, YC * j : YC * (j + 1), :]
                new = old * jnp.exp(acc[p] / count)
                newf[it, p, YC * j : YC * (j + 1), :] = new
                if it < ITERS - 1:
                    ef[it + 1, PAD + mine + p, YC * j : YC * (j + 1), :] = new
            if it < ITERS - 1:
                target = ef.at[it + 1, pl.ds(PAD + mine, PIECE), rows]
            else:
                target = out_ref.at[0, pl.ds(mine, PIECE), rows]
                cp = pltpu.make_async_copy(newf.at[it, :, rows], target, lsem.at[3 + j])
                cp.start()
                vsent.append(cp)
            for i, (to, frm) in enumerate(peers):
                cp = pltpu.make_async_remote_copy(
                    src_ref=newf.at[it, :, rows], dst_ref=target,
                    send_sem=ag_s.at[it, i, j], recv_sem=ag_r.at[it, i, j],
                    device_id={"view": to}, device_id_type=MESH)
                cp.start()
                vsent.append(cp)

        def gather_step(j):
            rows = pl.ds(YC * j, YC)
            for i, (to, frm) in enumerate(peers):
                if it < ITERS - 1:
                    target = ef.at[it + 1, pl.ds(PAD + frm * PIECE, PIECE), rows]
                else:
                    target = out_ref.at[0, pl.ds(frm * PIECE, PIECE), rows]
                pltpu.make_async_remote_copy(
                    src_ref=newf.at[it, :, rows], dst_ref=target,
                    send_sem=ag_s.at[it, i, j], recv_sem=ag_r.at[it, i, j],
                    device_id={"view": to}, device_id_type=MESH).wait_recv()
            if it < ITERS - 1:
                send_z(estimate_rims(it + 1, j))

        for n in range(NJ + 6):
            if n < NJ:
                log_step(ORDER[n])
            if 0 <= n - 2 < NJ:
                sum_step(ORDER[n - 2])
            if 0 <= n - 4 < NJ:
                gather_step(ORDER[n - 4])
            if 0 <= n - 6 < NJ and it < ITERS - 1:
                j = ORDER[n - 6]
                wait_recv(estimate_rims(it + 1, j), has_zlo, has_zhi)
                blur_rows(it + 1, YC * j, YC)

    for pair in zsent:
        wait_send(pair, has_zlo, has_zhi)
    for cond, cp in ysent:

        @pl.when(cond)
        def _():
            cp.wait_send()

    for cp in vsent:
        if cp.is_remote:
            cp.wait_send()
        else:
            cp.wait()


def body(estimate, views_data, psf_taps, view_bounds):
    dma = pltpu.SemaphoreType.DMA
    return pl.pallas_call(
        kernel,
        out_shape=jax.ShapeDtypeStruct(estimate.shape, F32),
        in_specs=[
            pl.BlockSpec(memory_space=pltpu.SMEM),
            pl.BlockSpec(memory_space=pltpu.HBM),
            pl.BlockSpec(memory_space=pltpu.HBM),
            pl.BlockSpec(memory_space=pltpu.HBM),
        ],
        out_specs=pl.BlockSpec(memory_space=pl.ANY),
        scratch_shapes=[
            pltpu.VMEM((ITERS, 64, Y, X), F32),
            pltpu.VMEM((ITERS, Z, 80, X), F32),
            pltpu.VMEM((ITERS, Z, 80, X), F32),
            pltpu.VMEM((ITERS, 64, Y, X), F32),
            pltpu.VMEM((ITERS, Z, Y, X), F32),
            pltpu.VMEM((ITERS, VIEWS - 1, PIECE, Y, X), F32),
            pltpu.VMEM((ITERS, PIECE, Y, X), F32),
            pltpu.VMEM((Z, Y, X), F32),
            pltpu.VMEM((Z, Y, X), F32),
            pltpu.VMEM((3, 1, TAPS), F32),
            pltpu.VMEM((2, 256, 1536), BF16),
            pltpu.VMEM((2, Y, 256), BF16),
            pltpu.VMEM((2, 2 * PAD, 128), BF16),
            pltpu.VMEM((2, 256, 256), BF16),
            dma((3 + NJ,)),
            dma((ITERS, 2, 2, NJ)),
            dma((ITERS, 2, 2, NJ)),
            dma((1, 2, FIRST_NJ)),
            dma((1, 2, FIRST_NJ)),
            dma((2, VIEWS - 1, FIRST_NJ)),
            dma((2, VIEWS - 1, FIRST_NJ)),
            dma((ITERS, 2, 2, NZC)),
            dma((ITERS, 2, 2, NZC)),
            dma((ITERS, VIEWS - 1, NJ)),
            dma((ITERS, VIEWS - 1, NJ)),
            dma((ITERS, VIEWS - 1, NJ)),
            dma((ITERS, VIEWS - 1, NJ)),
        ],
        compiler_params=pltpu.CompilerParams(
            collective_id=0, has_side_effects=True, vmem_limit_bytes=64000000
        ),
        name="deconvolve",
    )(view_bounds.T, psf_taps.transpose(1, 0, 2), estimate, views_data)


def solution(mesh):
    return jax.shard_map(
        body,
        mesh=mesh,
        in_specs=(
            P("block", None, None, None),
            P("view", "block", None, None, None),
            P("view", None, None),
            P(),
        ),
        out_specs=P("block", None, None, None),
        check_vma=False,
    )
```

```python
import functools

import jax
import jax.numpy as jnp
from jax import lax
from jax.experimental import pallas as pl
from jax.experimental.pallas import tpu as pltpu
from jax.sharding import PartitionSpec as P

MESH = pl.DeviceIdType.MESH
F32 = jnp.float32
BF16 = jnp.bfloat16

BY = 4
ITERS = 2
Z, Y, X = 32, 48, 128
TAPS = 31
HALF = 15
PAD = 16
VIEW_X, VIEW_Y = 4, 2
VIEWS = VIEW_X * VIEW_Y
PIECE = Z // VIEWS
CHUNKS = ((16, 16), (0, 16), (32, 8), (40, 8))
NJ = len(CHUNKS)
FIRST_YC = 16
FIRST_NJ = Y // FIRST_YC
FIRST = (0, 2, 1)
S1, S2, S3 = 3, 5, 7
ZC = 8
NZC = Z // ZC
ZORDER = (0, 3, 1, 2)


def split(x):
    hi = x.astype(BF16)
    lo = (x - hi.astype(F32)).astype(BF16)
    return hi, lo


def fill_tap(offset, taps, flip):
    acc = jnp.zeros(offset.shape, F32)
    for k in range(TAPS):
        at = TAPS - 1 - k if flip else k
        acc = jnp.where(offset == k, taps[:, at : at + 1], acc)
    return acc


def own_plane(slot):
    return (slot >> 2) + VIEWS * (slot & 3)


def estimate_plane(slot):
    z = own_plane(slot & (Z - 1))
    return jnp.where(slot < Z, z, jnp.where((slot & 3) < 2, z + Z, z - Z))


def build_z(taps, kz_ref, f):
    def z_rows(i, _):
        r0 = pl.multiple_of(i * 16, 16)
        row = lax.broadcasted_iota(jnp.int32, (16, 512), 0) + r0
        col = lax.broadcasted_iota(jnp.int32, (16, 512), 1)
        if f == 0:
            source, target = estimate_plane(col >> 3), row >> 3
        else:
            source, target = (col >> 3) - PAD, own_plane(row >> 3)
        k = jnp.where((col & 7) == (row & 7), source - target + HALF, -1)
        hi, lo = split(fill_tap(k, taps[0], f == 1))
        kz_ref[f, pl.ds(r0, 16), 0:512] = hi
        kz_ref[f, pl.ds(r0, 16), 512:1024] = hi
        kz_ref[f, pl.ds(r0, 16), 1024:1536] = lo
        return 0

    lax.fori_loop(0, 16, z_rows, 0)


def build_xy(taps, ko_ref, kr_ref, wx_ref, f):
    row = lax.broadcasted_iota(jnp.int32, (Y, 256), 0)
    col = lax.broadcasted_iota(jnp.int32, (Y, 256), 1)
    part = jnp.where(col >= 96, 2, jnp.where(col >= 48, 1, 0))
    k = jnp.where(col < 144, col - 48 * part - row + HALF, -1)
    val = fill_tap(k, taps[1], f == 1)
    hi = val.astype(BF16).astype(F32)
    ko_ref[f] = jnp.where(part == 2, val - hi, hi).astype(BF16)

    row = lax.broadcasted_iota(jnp.int32, (2 * PAD, 128), 0)
    col = lax.broadcasted_iota(jnp.int32, (2 * PAD, 128), 1)
    part = jnp.where(col >= 64, 2, jnp.where(col >= 32, 1, 0))
    at = col - 32 * part
    source = jnp.where(at < PAD, at - PAD, at + Y - PAD)
    target = jnp.where(row < PAD, row, row + Y - 2 * PAD)
    k = jnp.where(col < 96, source - target + HALF, -1)
    val = fill_tap(k, taps[1], f == 1)
    hi = val.astype(BF16).astype(F32)
    kr_ref[f] = jnp.where(part == 2, val - hi, hi).astype(BF16)

    def x_rows(i, _):
        r0 = pl.multiple_of(i * 16, 16)
        row = lax.broadcasted_iota(jnp.int32, (16, 128), 0) + r0
        col = lax.broadcasted_iota(jnp.int32, (16, 128), 1)
        hi, lo = split(fill_tap(row - col + HALF, taps[2], f == 1))
        wx_ref[f, pl.ds(r0, 16), 0:128] = hi
        wx_ref[f, pl.ds(r0, 16), 128:256] = lo
        r1 = pl.multiple_of(r0 + 128, 16)
        wx_ref[f, pl.ds(r1, 16), 0:128] = hi
        wx_ref[f, pl.ds(r1, 16), 128:256] = jnp.zeros((16, 128), BF16)
        return 0

    lax.fori_loop(0, 8, x_rows, 0)


def z_blur(ext, kz):
    cols = [ext[:, 8 * g : 8 * g + 8, :].reshape(64 * 8, X) for g in range(ext.shape[1] // 8)]
    hi, lo = split(jnp.concatenate(cols, axis=1))
    stack = jnp.concatenate([hi, lo, hi], axis=0)
    return jnp.dot(kz, stack, preferred_element_type=F32)


def y_blur(planes, ky):
    hi, lo = split(jnp.concatenate(planes, axis=1))
    stack = jnp.concatenate([hi, lo, hi], axis=0)
    return jnp.dot(ky, stack, preferred_element_type=F32)


def x_blur(rows, wx):
    hi, lo = split(rows)
    out = jnp.dot(jnp.concatenate([hi, lo], axis=1), wx, preferred_element_type=F32)
    return out[:, :X] + out[:, X:]


def kernel(
    bounds_ref, taps_ref, est_ref, data_ref, out_ref,
    ef, ya, rb, eb, lg, rr, newf, dv, pa, taps_v, kz, ko, kr, wx,
    lsem, zs, zr, ds, dr, ms, mr, hs, hr, fs, fr, ys, yr, rs_s, rs_r, ag_s, ag_r,
):
    b = lax.axis_index("block")
    v = lax.axis_index("view")
    vx, vy = lax.rem(v, VIEW_X), lax.div(v, VIEW_X)
    bz, by = lax.div(b, BY), lax.rem(b, BY)
    n_bz = lax.axis_size("block") // BY
    has_zlo, has_zhi = bz > 0, bz < n_bz - 1
    has_ylo, has_yhi = by > 0, by < BY - 1

    peers = []
    for dy in range(VIEW_Y):
        for dx in range(VIEW_X):
            if dx or dy:
                to = lax.rem(vy + dy, VIEW_Y) * VIEW_X + lax.rem(vx + dx, VIEW_X)
                frm = lax.rem(vy + VIEW_Y - dy, VIEW_Y) * VIEW_X + lax.rem(vx + VIEW_X - dx, VIEW_X)
                peers.append((to, frm))

    load_est = [
        pltpu.make_async_copy(est_ref.at[0, m], ef.at[0, pl.ds(0, VIEWS), m], lsem.at[3 + NJ + m])
        for m in range(PIECE)
    ]
    load_data = pltpu.make_async_copy(data_ref.at[0, 0], dv, lsem.at[1])
    load_taps = pltpu.make_async_copy(taps_ref, taps_v, lsem.at[2])
    for cp in load_est:
        cp.start()
    load_data.start()
    load_taps.start()

    bar = pltpu.get_barrier_semaphore()
    total = jnp.int32(VIEWS - 1)
    for cond, dst in ((has_zlo, b - BY), (has_zhi, b + BY), (has_ylo, b - 1), (has_yhi, b + 1)):
        total = total + cond.astype(jnp.int32)

        @pl.when(cond)
        def _():
            pl.semaphore_signal(bar, inc=1, device_id={"block": dst}, device_id_type=MESH)

    for to, _ in peers:
        pl.semaphore_signal(bar, inc=1, device_id={"view": to}, device_id_type=MESH)

    for it in range(ITERS):
        eb[it, 0] = jnp.zeros((Y, X), F32)
        eb[it, 63] = jnp.zeros((Y, X), F32)

        @pl.when(jnp.logical_not(has_zlo))
        def _():
            eb[it, 1:PAD] = jnp.zeros((HALF, Y, X), F32)

        @pl.when(jnp.logical_not(has_zhi))
        def _():
            eb[it, PAD + Z : PAD + Z + HALF] = jnp.zeros((HALF, Y, X), F32)

        for cond, members in ((has_zhi, (0, 1)), (has_zlo, (3, 2))):

            @pl.when(jnp.logical_not(cond))
            def _():
                for m in members:
                    ef[it, VIEWS + v, m] = jnp.zeros((Y, X), F32)
                if it == 0:
                    for g in range(VIEWS):
                        ef[it, VIEWS + g, members[0]] = jnp.zeros((Y, X), F32)

        for buf in (ya, rb):

            @pl.when(jnp.logical_not(has_ylo))
            def _():
                buf[it, :, 0:PAD, :] = jnp.zeros((Z, PAD, X), F32)

            @pl.when(jnp.logical_not(has_yhi))
            def _():
                buf[it, :, PAD + Y :, :] = jnp.zeros((Z, PAD, X), F32)

    for cp in load_est:
        cp.wait()
    pl.semaphore_wait(bar, total)

    def z_pair(up, down, sems, recvs, key):
        out = []
        for d, (src, dst) in enumerate((up, down)):
            out.append(pltpu.make_async_remote_copy(
                src_ref=src, dst_ref=dst, send_sem=sems.at[(d,) + key], recv_sem=recvs.at[(d,) + key],
                device_id={"block": b - BY if d else b + BY}, device_id_type=MESH))
        return out

    def ratio_rims(it, j):
        rows = pl.ds(*CHUNKS[j])
        return z_pair(
            (eb.at[it, pl.ds(PAD + Z - HALF, HALF), rows], eb.at[it, pl.ds(1, HALF), rows]),
            (eb.at[it, pl.ds(PAD, HALF), rows], eb.at[it, pl.ds(PAD + Z, HALF), rows]),
            zs, zr, (it, j))

    def middle_rims(it, part):
        rows = pl.ds(*CHUNKS[0])
        up = ((PAD + 24, 8, 8), (PAD + 17, 1, 7))[part]
        down = ((PAD, PAD + Z, 8), (PAD + 8, PAD + Z + 8, 7))[part]
        return z_pair(
            *((eb.at[it, pl.ds(a, k), rows], eb.at[it, pl.ds(c, k), rows]) for a, c, k in (up, down)),
            ms, mr, (it, part))

    def direct_rims(j):
        rows = pl.ds(FIRST_YC * j, FIRST_YC)
        source, target = pl.ds(0, VIEWS), pl.ds(VIEWS, VIEWS)
        return z_pair(
            (ef.at[0, source, 3, rows], ef.at[0, target, 3, rows]),
            (ef.at[0, source, 0, rows], ef.at[0, target, 0, rows]),
            ds, dr, (j,))

    def shared_rims(j):
        rows = pl.ds(FIRST_YC * j, FIRST_YC)
        return z_pair(
            (ef.at[0, v, pl.ds(2, 1), rows], ef.at[0, VIEWS + v, pl.ds(2, 1), rows]),
            (ef.at[0, v, pl.ds(1, 1), rows], ef.at[0, VIEWS + v, pl.ds(1, 1), rows]),
            hs, hr, (0, j))

    def owned_rims(it, j):
        rows = pl.ds(*CHUNKS[j])
        return z_pair(
            (newf.at[it - 1, pl.ds(2, 2), rows], ef.at[it, VIEWS + v, pl.ds(2, 2), rows]),
            (newf.at[it - 1, pl.ds(0, 2), rows], ef.at[it, VIEWS + v, pl.ds(0, 2), rows]),
            hs, hr, (it, j))

    def forwards(it, j, outgoing):
        rows = pl.ds(*CHUNKS[j]) if it else pl.ds(FIRST_YC * j, FIRST_YC)
        members = pl.ds(0, 4) if it else pl.ds(1, 2)
        out = []
        for i, (to, frm) in enumerate(peers):
            part = ef.at[it, VIEWS + (v if outgoing else frm), members, rows]
            out.append(pltpu.make_async_remote_copy(
                src_ref=part, dst_ref=part, send_sem=fs.at[it, i, j], recv_sem=fr.at[it, i, j],
                device_id={"view": to}, device_id_type=MESH))
        return out

    def forward(it, j):
        for cp in forwards(it, j, True):
            cp.start()
            vsent.append(cp)

    def wait_forwards(it, j):
        for cp in forwards(it, j, False):
            cp.wait_recv()

    def y_pair(buf, it, which, planes, n, c, half):
        up = pltpu.make_async_remote_copy(
            src_ref=buf.at[it, planes, pl.ds(Y + half, n)], dst_ref=buf.at[it, planes, pl.ds(half, n)],
            send_sem=ys.at[it, which, 0, c], recv_sem=yr.at[it, which, 0, c],
            device_id={"block": b + 1}, device_id_type=MESH)
        down = pltpu.make_async_remote_copy(
            src_ref=buf.at[it, planes, pl.ds(PAD + half, n)], dst_ref=buf.at[it, planes, pl.ds(PAD + Y + half, n)],
            send_sem=ys.at[it, which, 1, c], recv_sem=yr.at[it, which, 1, c],
            device_id={"block": b - 1}, device_id_type=MESH)
        return up, down

    def blurred_rims(it, h):
        return y_pair(ya, it, 0, pl.ds(0, Z), 8, h, 8 * h)

    def ratio_y_rims(it, c):
        return y_pair(rb, it, 1, pl.ds(ZC * c, ZC), PAD, c, 0)

    def start(pair, lo, hi):
        up, down = pair

        @pl.when(hi)
        def _():
            up.start()

        @pl.when(lo)
        def _():
            down.start()

    def wait_recv(pair, lo, hi):
        up, down = pair

        @pl.when(lo)
        def _():
            up.wait_recv()

        @pl.when(hi)
        def _():
            down.wait_recv()

    def wait_send(pair, lo, hi):
        up, down = pair

        @pl.when(hi)
        def _():
            up.wait_send()

        @pl.when(lo)
        def _():
            down.wait_send()

    zsent, ysent, vsent = [], [], []

    def send_z(pair):
        start(pair, has_zlo, has_zhi)
        zsent.append(pair)

    def send_y(up, down):
        if up is not None:

            @pl.when(has_yhi)
            def _():
                up.start()

            ysent.append((has_yhi, up))
        if down is not None:

            @pl.when(has_ylo)
            def _():
                down.start()

            ysent.append((has_ylo, down))

    def start_up(pair):
        @pl.when(has_zhi)
        def _():
            pair[0].start()

    def start_down(pair):
        @pl.when(has_zlo)
        def _():
            pair[1].start()

    for j in FIRST:
        send_z(shared_rims(j))
    for j in FIRST:
        send_z(direct_rims(j))

    load_taps.wait()
    taps = taps_v[...]
    taps = taps / jnp.sum(taps, axis=2, keepdims=True)
    build_z(taps, kz, 0)

    z0, y0 = bz * Z, by * Y
    ypos = lax.broadcasted_iota(jnp.int32, (Y, X), 0) + y0
    own_y = jnp.where((ypos >= bounds_ref[2, v]) & (ypos < bounds_ref[3, v]), 1.0, 0.0).astype(F32)

    def own_z(plane):
        zpos = z0 + plane
        return (zpos >= bounds_ref[0, v]) & (zpos < bounds_ref[1, v])

    def blur_rows(it, r0, rows):
        res = z_blur(ef[it, :, :, r0 : r0 + rows, :].reshape(64, rows, X), kz[0])
        for r in range(r0, r0 + rows, 8):
            at = X * ((r - r0) // 8)
            ya[it, :, PAD + r : PAD + r + 8, :] = res[:, at : at + X].reshape(Z, 8, X)
            if r < PAD:
                send_y(None, blurred_rims(it, r // 8)[1])
            if r >= Y - PAD:
                send_y(blurred_rims(it, (r - Y + PAD) // 8)[0], None)

    for j in FIRST:
        wait_recv(shared_rims(j), has_zlo, has_zhi)
        forward(0, j)
    build_xy(taps, ko, kr, wx, 0)
    build_xy(taps, ko, kr, wx, 1)
    build_z(taps, kz, 1)
    load_data.wait()
    for j in FIRST:
        wait_recv(direct_rims(j), has_zlo, has_zhi)
        wait_forwards(0, j)
        blur_rows(0, FIRST_YC * j, FIRST_YC)

    for it in range(ITERS):
        own = slice(PAD, PAD + Y)
        for p in range(0, Z, 2):
            res = y_blur([ya[it, p, own], ya[it, p + 1, own]], ko[0][:, :144])
            pa[p] = res[:, :X]
            pa[p + 1] = res[:, X:]
        for h in range(2):
            wait_recv(blurred_rims(it, h), has_ylo, has_yhi)

        def rims(buf, p):
            return jnp.concatenate([buf[it, p, 0:PAD], buf[it, p, PAD + Y :]], axis=0)

        for c in ZORDER:
            span = range(ZC * c, ZC * (c + 1), 2)
            parts = []
            for p in span:
                res = y_blur([rims(ya, p), rims(ya, p + 1)], kr[0][:, :96])
                for h in range(2):
                    edge = res[:, X * h : X * (h + 1)]
                    parts += [pa[p + h, 0:PAD] + edge[:PAD], pa[p + h, PAD : 2 * PAD], pa[p + h, 2 * PAD :] + edge[PAD:]]
            blurred = x_blur(jnp.concatenate(parts, axis=0), wx[0])
            ratio = dv[ZC * c : ZC * (c + 1)].reshape(ZC * Y, X) / blurred
            rb[it, ZC * c : ZC * (c + 1), own, :] = x_blur(ratio, wx[1]).reshape(ZC, Y, X)
            send_y(*ratio_y_rims(it, c))
            for p in span:
                res = y_blur([rb[it, p, own], rb[it, p + 1, own]], ko[1][:, :144])
                eb[it, PAD + p] = res[:, :X]
                eb[it, PAD + p + 1] = res[:, X:]
            pair = middle_rims(it, 0 if c in (0, 3) else 1)
            if c < NZC // 2:
                start_down(pair)
                zsent.append(pair)
            else:
                start_up(pair)
        for c in ZORDER:
            wait_recv(ratio_y_rims(it, c), has_ylo, has_yhi)
            for p in range(ZC * c, ZC * (c + 1), 2):
                res = y_blur([rims(rb, p), rims(rb, p + 1)], kr[1][:, :96])
                for h in range(2):
                    edge = res[:, X * h : X * (h + 1)]
                    eb[it, PAD + p + h, 0:PAD] += edge[:PAD]
                    eb[it, PAD + p + h, 2 * PAD :] += edge[PAD:]
            if c == ZORDER[2]:
                for j in range(1, NJ):
                    pair = ratio_rims(it, j)
                    zsent.append(pair)
                    start_down(pair)
        for j in range(1, NJ):
            start_up(ratio_rims(it, j))

        mine = v * PIECE

        def log_step(j):
            if j:
                wait_recv(ratio_rims(it, j), has_zlo, has_zhi)
            else:
                for part in range(2):
                    wait_recv(middle_rims(it, part), has_zlo, has_zhi)
            r0, n = CHUNKS[j]
            res = z_blur(eb[it, :, r0 : r0 + n, :], kz[1])
            for g in range(n // 8):
                r = r0 + 8 * g
                logs = jnp.log(res[:, X * g : X * (g + 1)].reshape(Z, 8, X))
                for p in range(Z):
                    keep = jnp.where(own_z(own_plane(p)), own_y[r : r + 8], 0.0)
                    lg[it, p, r : r + 8, :] = keep * logs[p]
            rows = pl.ds(*CHUNKS[j])
            for i, (to, frm) in enumerate(peers):
                cp = pltpu.make_async_remote_copy(
                    src_ref=lg.at[it, pl.ds(to * PIECE, PIECE), rows],
                    dst_ref=rr.at[it, i, :, rows],
                    send_sem=rs_s.at[it, i, j], recv_sem=rs_r.at[it, i, j],
                    device_id={"view": to}, device_id_type=MESH)
                cp.start()
                vsent.append(cp)

        def sum_step(j):
            rows = pl.ds(*CHUNKS[j])
            r0, n = CHUNKS[j]
            acc = lg[it, pl.ds(mine, PIECE), r0 : r0 + n, :]
            for i in range(VIEWS - 1):
                pltpu.make_async_remote_copy(
                    src_ref=lg.at[it, pl.ds(0, PIECE), rows], dst_ref=rr.at[it, i, :, rows],
                    send_sem=rs_s.at[it, i, j], recv_sem=rs_r.at[it, i, j],
                    device_id={"view": peers[i][0]}, device_id_type=MESH).wait_recv()
                acc = acc + rr[it, i, :, r0 : r0 + n, :]
            yj = ypos[r0 : r0 + n]
            ins = [
                jnp.where((yj >= bounds_ref[2, w]) & (yj < bounds_ref[3, w]), 1.0, 0.0).astype(F32)
                for w in range(VIEWS)
            ]
            for p in range(PIECE):
                zpos = z0 + v + VIEWS * p
                count = jnp.zeros((n, X), F32)
                for w in range(VIEWS):
                    inz = (zpos >= bounds_ref[0, w]) & (zpos < bounds_ref[1, w])
                    count = count + jnp.where(inz, ins[w], 0.0)
                old = ef[it, v, p, r0 : r0 + n, :]
                new = old * jnp.exp(acc[p] / count)
                newf[it, p, r0 : r0 + n, :] = new
                if it < ITERS - 1:
                    ef[it + 1, v, p, r0 : r0 + n, :] = new
            if it < ITERS - 1:
                target = ef.at[it + 1, v, :, rows]
                send_z(owned_rims(it + 1, j))
            else:
                target = out_ref.at[0, :, v, rows]
                cp = pltpu.make_async_copy(newf.at[it, :, rows], target, lsem.at[3 + j])
                cp.start()
                vsent.append(cp)
            for i, (to, frm) in enumerate(peers):
                cp = pltpu.make_async_remote_copy(
                    src_ref=newf.at[it, :, rows], dst_ref=target,
                    send_sem=ag_s.at[it, i, j], recv_sem=ag_r.at[it, i, j],
                    device_id={"view": to}, device_id_type=MESH)
                cp.start()
                vsent.append(cp)

        def gather_step(j):
            rows = pl.ds(*CHUNKS[j])
            for i, (to, frm) in enumerate(peers):
                if it < ITERS - 1:
                    target = ef.at[it + 1, frm, :, rows]
                else:
                    target = out_ref.at[0, :, frm, rows]
                pltpu.make_async_remote_copy(
                    src_ref=newf.at[it, :, rows], dst_ref=target,
                    send_sem=ag_s.at[it, i, j], recv_sem=ag_r.at[it, i, j],
                    device_id={"view": to}, device_id_type=MESH).wait_recv()

        for n in range(NJ + S3):
            if n < NJ:
                log_step(n)
            if 0 <= n - S1 < NJ:
                sum_step(n - S1)
            if it < ITERS - 1:
                if 0 <= n - S2 < NJ:
                    j = n - S2
                    wait_recv(owned_rims(it + 1, j), has_zlo, has_zhi)
                    forward(it + 1, j)
                if 0 <= n - S3 < NJ:
                    j = n - S3
                    gather_step(j)
                    wait_forwards(it + 1, j)
                    blur_rows(it + 1, *CHUNKS[j])
        if it == ITERS - 1:
            for j in range(NJ):
                gather_step(j)

    for pair in zsent:
        wait_send(pair, has_zlo, has_zhi)
    for cond, cp in ysent:

        @pl.when(cond)
        def _():
            cp.wait_send()

    for cp in vsent:
        if cp.is_remote:
            cp.wait_send()
        else:
            cp.wait()


def body(estimate, views_data, psf_taps, view_bounds):
    dma = pltpu.SemaphoreType.DMA
    return pl.pallas_call(
        kernel,
        out_shape=pltpu.VMEM((1, PIECE, VIEWS, Y, X), F32),
        in_specs=[
            pl.BlockSpec(memory_space=pltpu.SMEM),
            pl.BlockSpec(memory_space=pltpu.HBM),
            pl.BlockSpec(memory_space=pltpu.HBM),
            pl.BlockSpec(memory_space=pltpu.HBM),
        ],
        out_specs=pl.BlockSpec(memory_space=pltpu.VMEM),
        scratch_shapes=[
            pltpu.VMEM((ITERS, 16, PIECE, Y, X), F32),
            pltpu.VMEM((ITERS, Z, 80, X), F32),
            pltpu.VMEM((ITERS, Z, 80, X), F32),
            pltpu.VMEM((ITERS, 64, Y, X), F32),
            pltpu.VMEM((ITERS, Z, Y, X), F32),
            pltpu.VMEM((ITERS, VIEWS - 1, PIECE, Y, X), F32),
            pltpu.VMEM((ITERS, PIECE, Y, X), F32),
            pltpu.VMEM((Z, Y, X), F32),
            pltpu.VMEM((Z, Y, X), F32),
            pltpu.VMEM((3, 1, TAPS), F32),
            pltpu.VMEM((2, 256, 1536), BF16),
            pltpu.VMEM((2, Y, 256), BF16),
            pltpu.VMEM((2, 2 * PAD, 128), BF16),
            pltpu.VMEM((2, 256, 256), BF16),
            dma((3 + NJ + PIECE,)),
            dma((2, ITERS, NJ)),
            dma((2, ITERS, NJ)),
            dma((2, FIRST_NJ)),
            dma((2, FIRST_NJ)),
            dma((2, ITERS, 2)),
            dma((2, ITERS, 2)),
            dma((2, ITERS, NJ)),
            dma((2, ITERS, NJ)),
            dma((ITERS, VIEWS - 1, NJ)),
            dma((ITERS, VIEWS - 1, NJ)),
            dma((ITERS, 2, 2, NZC)),
            dma((ITERS, 2, 2, NZC)),
            dma((ITERS, VIEWS - 1, NJ)),
            dma((ITERS, VIEWS - 1, NJ)),
            dma((ITERS, VIEWS - 1, NJ)),
            dma((ITERS, VIEWS - 1, NJ)),
        ],
        compiler_params=pltpu.CompilerParams(
            collective_id=0, has_side_effects=True, vmem_limit_bytes=60000000
        ),
        name="deconvolve",
    )(view_bounds.T, psf_taps.transpose(1, 0, 2), estimate.reshape(1, PIECE, VIEWS, Y, X), views_data).reshape(estimate.shape)


def solution(mesh):
    return jax.shard_map(
        body,
        mesh=mesh,
        in_specs=(
            P("block", None, None, None),
            P("view", "block", None, None, None),
            P("view", None, None),
            P(),
        ),
        out_specs=P("block", None, None, None),
        check_vma=False,
    )
```

```python
import functools

import jax
import jax.numpy as jnp
from jax import lax
from jax.experimental import pallas as pl
from jax.experimental.pallas import tpu as pltpu
from jax.sharding import PartitionSpec as P

MESH = pl.DeviceIdType.MESH
F32 = jnp.float32
BF16 = jnp.bfloat16

BY = 4
ITERS = 2
Z, Y, X = 32, 48, 128
TAPS = 31
HALF = 15
PAD = 16
VIEW_X, VIEW_Y = 4, 2
VIEWS = VIEW_X * VIEW_Y
PIECE = Z // VIEWS
CHUNKS = ((16, 8), (24, 8), (0, 16), (32, 8), (40, 8))
MIDDLE = 2
PROC = ((0, 2, 3, 4, 1), (0, 1, 2, 3, 4))
NJ = len(CHUNKS)
FIRST_YC = 16
FIRST_NJ = Y // FIRST_YC
FIRST = (0, 2, 1)
S1, S2, S3 = 4, 7, 9
ZC = 8
NZC = Z // ZC
ZORDER = (0, 3, 1, 2)


def split(x):
    hi = x.astype(BF16)
    lo = (x - hi.astype(F32)).astype(BF16)
    return hi, lo


def fill_tap(offset, taps, flip):
    acc = jnp.zeros(offset.shape, F32)
    for k in range(TAPS):
        at = TAPS - 1 - k if flip else k
        acc = jnp.where(offset == k, taps[:, at : at + 1], acc)
    return acc


def own_plane(slot):
    return (slot >> 2) + VIEWS * (slot & 3)


def estimate_plane(slot):
    z = own_plane(slot & (Z - 1))
    return jnp.where(slot < Z, z, jnp.where((slot & 3) < 2, z + Z, z - Z))


def build_z(taps, kz_ref, f):
    def z_rows(i, _):
        r0 = pl.multiple_of(i * 16, 16)
        row = lax.broadcasted_iota(jnp.int32, (16, 512), 0) + r0
        col = lax.broadcasted_iota(jnp.int32, (16, 512), 1)
        if f == 0:
            source, target = estimate_plane(col >> 3), row >> 3
        else:
            source, target = (col >> 3) - PAD, own_plane(row >> 3)
        k = jnp.where((col & 7) == (row & 7), source - target + HALF, -1)
        hi, lo = split(fill_tap(k, taps[0], f == 1))
        kz_ref[f, pl.ds(r0, 16), 0:512] = hi
        kz_ref[f, pl.ds(r0, 16), 512:1024] = hi
        kz_ref[f, pl.ds(r0, 16), 1024:1536] = lo
        return 0

    lax.fori_loop(0, 16, z_rows, 0)


def build_xy(taps, ko_ref, kr_ref, wx_ref, f):
    row = lax.broadcasted_iota(jnp.int32, (Y, 256), 0)
    col = lax.broadcasted_iota(jnp.int32, (Y, 256), 1)
    part = jnp.where(col >= 96, 2, jnp.where(col >= 48, 1, 0))
    k = jnp.where(col < 144, col - 48 * part - row + HALF, -1)
    val = fill_tap(k, taps[1], f == 1)
    hi = val.astype(BF16).astype(F32)
    ko_ref[f] = jnp.where(part == 2, val - hi, hi).astype(BF16)

    row = lax.broadcasted_iota(jnp.int32, (2 * PAD, 128), 0)
    col = lax.broadcasted_iota(jnp.int32, (2 * PAD, 128), 1)
    part = jnp.where(col >= 64, 2, jnp.where(col >= 32, 1, 0))
    at = col - 32 * part
    source = jnp.where(at < PAD, at - PAD, at + Y - PAD)
    target = jnp.where(row < PAD, row, row + Y - 2 * PAD)
    k = jnp.where(col < 96, source - target + HALF, -1)
    val = fill_tap(k, taps[1], f == 1)
    hi = val.astype(BF16).astype(F32)
    kr_ref[f] = jnp.where(part == 2, val - hi, hi).astype(BF16)

    def x_rows(i, _):
        r0 = pl.multiple_of(i * 16, 16)
        row = lax.broadcasted_iota(jnp.int32, (16, 128), 0) + r0
        col = lax.broadcasted_iota(jnp.int32, (16, 128), 1)
        hi, lo = split(fill_tap(row - col + HALF, taps[2], f == 1))
        wx_ref[f, pl.ds(r0, 16), 0:128] = hi
        wx_ref[f, pl.ds(r0, 16), 128:256] = lo
        r1 = pl.multiple_of(r0 + 128, 16)
        wx_ref[f, pl.ds(r1, 16), 0:128] = hi
        wx_ref[f, pl.ds(r1, 16), 128:256] = jnp.zeros((16, 128), BF16)
        return 0

    lax.fori_loop(0, 8, x_rows, 0)


def z_blur(ext, kz):
    cols = [ext[:, 8 * g : 8 * g + 8, :].reshape(64 * 8, X) for g in range(ext.shape[1] // 8)]
    hi, lo = split(jnp.concatenate(cols, axis=1))
    stack = jnp.concatenate([hi, lo, hi], axis=0)
    return jnp.dot(kz, stack, preferred_element_type=F32)


def y_blur(planes, ky):
    hi, lo = split(jnp.concatenate(planes, axis=1))
    stack = jnp.concatenate([hi, lo, hi], axis=0)
    return jnp.dot(ky, stack, preferred_element_type=F32)


def x_blur(rows, wx):
    hi, lo = split(rows)
    out = jnp.dot(jnp.concatenate([hi, lo], axis=1), wx, preferred_element_type=F32)
    return out[:, :X] + out[:, X:]


def kernel(
    bounds_ref, taps_ref, est_ref, data_ref, out_ref,
    ef, ya, rb, eb, lg, rr, newf, dv, pa, taps_v, kz, ko, kr, wx,
    lsem, zs, zr, ds, dr, ms, mr, hs, hr, fs, fr, ys, yr, rs_s, rs_r, ag_s, ag_r,
):
    b = lax.axis_index("block")
    v = lax.axis_index("view")
    vx, vy = lax.rem(v, VIEW_X), lax.div(v, VIEW_X)
    bz, by = lax.div(b, BY), lax.rem(b, BY)
    n_bz = lax.axis_size("block") // BY
    has_zlo, has_zhi = bz > 0, bz < n_bz - 1
    has_ylo, has_yhi = by > 0, by < BY - 1

    peers = []
    for dy in range(VIEW_Y):
        for dx in range(VIEW_X):
            if dx or dy:
                to = lax.rem(vy + dy, VIEW_Y) * VIEW_X + lax.rem(vx + dx, VIEW_X)
                frm = lax.rem(vy + VIEW_Y - dy, VIEW_Y) * VIEW_X + lax.rem(vx + VIEW_X - dx, VIEW_X)
                peers.append((to, frm))

    load_est = [
        pltpu.make_async_copy(est_ref.at[0, m], ef.at[0, pl.ds(0, VIEWS), m], lsem.at[3 + NJ + m])
        for m in range(PIECE)
    ]
    load_data = pltpu.make_async_copy(data_ref.at[0, 0], dv, lsem.at[1])
    load_taps = pltpu.make_async_copy(taps_ref, taps_v, lsem.at[2])
    for cp in load_est:
        cp.start()
    load_data.start()
    load_taps.start()

    bar = pltpu.get_barrier_semaphore()
    total = jnp.int32(VIEWS - 1)
    for cond, dst in ((has_zlo, b - BY), (has_zhi, b + BY), (has_ylo, b - 1), (has_yhi, b + 1)):
        total = total + cond.astype(jnp.int32)

        @pl.when(cond)
        def _():
            pl.semaphore_signal(bar, inc=1, device_id={"block": dst}, device_id_type=MESH)

    for to, _ in peers:
        pl.semaphore_signal(bar, inc=1, device_id={"view": to}, device_id_type=MESH)

    for it in range(ITERS):
        eb[it, 0] = jnp.zeros((Y, X), F32)
        eb[it, 63] = jnp.zeros((Y, X), F32)

        @pl.when(jnp.logical_not(has_zlo))
        def _():
            eb[it, 1:PAD] = jnp.zeros((HALF, Y, X), F32)

        @pl.when(jnp.logical_not(has_zhi))
        def _():
            eb[it, PAD + Z : PAD + Z + HALF] = jnp.zeros((HALF, Y, X), F32)

        for cond, members in ((has_zhi, (0, 1)), (has_zlo, (3, 2))):

            @pl.when(jnp.logical_not(cond))
            def _():
                for m in members:
                    ef[it, VIEWS + v, m] = jnp.zeros((Y, X), F32)
                if it == 0:
                    for g in range(VIEWS):
                        ef[it, VIEWS + g, members[0]] = jnp.zeros((Y, X), F32)

        for buf in (ya, rb):

            @pl.when(jnp.logical_not(has_ylo))
            def _():
                buf[it, :, 0:PAD, :] = jnp.zeros((Z, PAD, X), F32)

            @pl.when(jnp.logical_not(has_yhi))
            def _():
                buf[it, :, PAD + Y :, :] = jnp.zeros((Z, PAD, X), F32)

    for cp in load_est:
        cp.wait()
    pl.semaphore_wait(bar, total)

    def z_pair(up, down, sems, recvs, key):
        out = []
        for d, (src, dst) in enumerate((up, down)):
            out.append(pltpu.make_async_remote_copy(
                src_ref=src, dst_ref=dst, send_sem=sems.at[(d,) + key], recv_sem=recvs.at[(d,) + key],
                device_id={"block": b - BY if d else b + BY}, device_id_type=MESH))
        return out

    def ratio_rims(it, j):
        rows = pl.ds(*CHUNKS[j])
        return z_pair(
            (eb.at[it, pl.ds(PAD + Z - HALF, HALF), rows], eb.at[it, pl.ds(1, HALF), rows]),
            (eb.at[it, pl.ds(PAD, HALF), rows], eb.at[it, pl.ds(PAD + Z, HALF), rows]),
            zs, zr, (it, j))

    def middle_rims(it, part):
        rows = pl.ds(16, 16)
        up = ((PAD + 24, 8, 8), (PAD + 17, 1, 7))[part]
        down = ((PAD, PAD + Z, 8), (PAD + 8, PAD + Z + 8, 7))[part]
        return z_pair(
            *((eb.at[it, pl.ds(a, k), rows], eb.at[it, pl.ds(c, k), rows]) for a, c, k in (up, down)),
            ms, mr, (it, part))

    def direct_rims(j):
        rows = pl.ds(FIRST_YC * j, FIRST_YC)
        source, target = pl.ds(0, VIEWS), pl.ds(VIEWS, VIEWS)
        return z_pair(
            (ef.at[0, source, 3, rows], ef.at[0, target, 3, rows]),
            (ef.at[0, source, 0, rows], ef.at[0, target, 0, rows]),
            ds, dr, (j,))

    def shared_rims(j):
        rows = pl.ds(FIRST_YC * j, FIRST_YC)
        return z_pair(
            (ef.at[0, v, pl.ds(2, 1), rows], ef.at[0, VIEWS + v, pl.ds(2, 1), rows]),
            (ef.at[0, v, pl.ds(1, 1), rows], ef.at[0, VIEWS + v, pl.ds(1, 1), rows]),
            hs, hr, (0, j))

    def owned_rims(it, j):
        rows = pl.ds(*CHUNKS[j])
        return z_pair(
            (newf.at[it - 1, pl.ds(2, 2), rows], ef.at[it, VIEWS + v, pl.ds(2, 2), rows]),
            (newf.at[it - 1, pl.ds(0, 2), rows], ef.at[it, VIEWS + v, pl.ds(0, 2), rows]),
            hs, hr, (it, j))

    def forwards(it, j, outgoing):
        rows = pl.ds(*CHUNKS[j]) if it else pl.ds(FIRST_YC * j, FIRST_YC)
        members = pl.ds(0, 4) if it else pl.ds(1, 2)
        out = []
        for i, (to, frm) in enumerate(peers):
            part = ef.at[it, VIEWS + (v if outgoing else frm), members, rows]
            out.append(pltpu.make_async_remote_copy(
                src_ref=part, dst_ref=part, send_sem=fs.at[it, i, j], recv_sem=fr.at[it, i, j],
                device_id={"view": to}, device_id_type=MESH))
        return out

    def forward(it, j):
        for cp in forwards(it, j, True):
            cp.start()
            vsent.append(cp)

    def wait_forwards(it, j):
        for cp in forwards(it, j, False):
            cp.wait_recv()

    def y_pair(buf, it, which, planes, n, c, half):
        up = pltpu.make_async_remote_copy(
            src_ref=buf.at[it, planes, pl.ds(Y + half, n)], dst_ref=buf.at[it, planes, pl.ds(half, n)],
            send_sem=ys.at[it, which, 0, c], recv_sem=yr.at[it, which, 0, c],
            device_id={"block": b + 1}, device_id_type=MESH)
        down = pltpu.make_async_remote_copy(
            src_ref=buf.at[it, planes, pl.ds(PAD + half, n)], dst_ref=buf.at[it, planes, pl.ds(PAD + Y + half, n)],
            send_sem=ys.at[it, which, 1, c], recv_sem=yr.at[it, which, 1, c],
            device_id={"block": b - 1}, device_id_type=MESH)
        return up, down

    def blurred_rims(it, h):
        return y_pair(ya, it, 0, pl.ds(0, Z), 8, h, 8 * h)

    def ratio_y_rims(it, c):
        return y_pair(rb, it, 1, pl.ds(ZC * c, ZC), PAD, c, 0)

    def start(pair, lo, hi):
        up, down = pair

        @pl.when(hi)
        def _():
            up.start()

        @pl.when(lo)
        def _():
            down.start()

    def wait_recv(pair, lo, hi):
        up, down = pair

        @pl.when(lo)
        def _():
            up.wait_recv()

        @pl.when(hi)
        def _():
            down.wait_recv()

    def wait_send(pair, lo, hi):
        up, down = pair

        @pl.when(hi)
        def _():
            up.wait_send()

        @pl.when(lo)
        def _():
            down.wait_send()

    zsent, ysent, vsent = [], [], []

    def send_z(pair):
        start(pair, has_zlo, has_zhi)
        zsent.append(pair)

    def send_y(up, down):
        if up is not None:

            @pl.when(has_yhi)
            def _():
                up.start()

            ysent.append((has_yhi, up))
        if down is not None:

            @pl.when(has_ylo)
            def _():
                down.start()

            ysent.append((has_ylo, down))

    def start_up(pair):
        @pl.when(has_zhi)
        def _():
            pair[0].start()

    def start_down(pair):
        @pl.when(has_zlo)
        def _():
            pair[1].start()

    for j in FIRST:
        send_z(shared_rims(j))
    for j in FIRST:
        send_z(direct_rims(j))

    load_taps.wait()
    taps = taps_v[...]
    taps = taps / jnp.sum(taps, axis=2, keepdims=True)
    build_z(taps, kz, 0)

    z0, y0 = bz * Z, by * Y
    ypos = lax.broadcasted_iota(jnp.int32, (Y, X), 0) + y0
    own_y = jnp.where((ypos >= bounds_ref[2, v]) & (ypos < bounds_ref[3, v]), 1.0, 0.0).astype(F32)

    def own_z(plane):
        zpos = z0 + plane
        return (zpos >= bounds_ref[0, v]) & (zpos < bounds_ref[1, v])

    def blur_rows(it, r0, rows):
        res = z_blur(ef[it, :, :, r0 : r0 + rows, :].reshape(64, rows, X), kz[0])
        for r in range(r0, r0 + rows, 8):
            at = X * ((r - r0) // 8)
            ya[it, :, PAD + r : PAD + r + 8, :] = res[:, at : at + X].reshape(Z, 8, X)
            if r < PAD:
                send_y(None, blurred_rims(it, r // 8)[1])
            if r >= Y - PAD:
                send_y(blurred_rims(it, (r - Y + PAD) // 8)[0], None)

    for j in FIRST:
        wait_recv(shared_rims(j), has_zlo, has_zhi)
        forward(0, j)
    build_xy(taps, ko, kr, wx, 0)
    build_xy(taps, ko, kr, wx, 1)
    build_z(taps, kz, 1)
    load_data.wait()
    for j in FIRST:
        wait_recv(direct_rims(j), has_zlo, has_zhi)
        wait_forwards(0, j)
        blur_rows(0, FIRST_YC * j, FIRST_YC)

    for it in range(ITERS):
        own = slice(PAD, PAD + Y)
        for p in range(0, Z, 2):
            res = y_blur([ya[it, p, own], ya[it, p + 1, own]], ko[0][:, :144])
            pa[p] = res[:, :X]
            pa[p + 1] = res[:, X:]
        for h in range(2):
            wait_recv(blurred_rims(it, h), has_ylo, has_yhi)

        def rims(buf, p):
            return jnp.concatenate([buf[it, p, 0:PAD], buf[it, p, PAD + Y :]], axis=0)

        for c in ZORDER:
            span = range(ZC * c, ZC * (c + 1), 2)
            parts = []
            for p in span:
                res = y_blur([rims(ya, p), rims(ya, p + 1)], kr[0][:, :96])
                for h in range(2):
                    edge = res[:, X * h : X * (h + 1)]
                    parts += [pa[p + h, 0:PAD] + edge[:PAD], pa[p + h, PAD : 2 * PAD], pa[p + h, 2 * PAD :] + edge[PAD:]]
            blurred = x_blur(jnp.concatenate(parts, axis=0), wx[0])
            ratio = dv[ZC * c : ZC * (c + 1)].reshape(ZC * Y, X) / blurred
            rb[it, ZC * c : ZC * (c + 1), own, :] = x_blur(ratio, wx[1]).reshape(ZC, Y, X)
            send_y(*ratio_y_rims(it, c))
            for p in span:
                res = y_blur([rb[it, p, own], rb[it, p + 1, own]], ko[1][:, :144])
                eb[it, PAD + p] = res[:, :X]
                eb[it, PAD + p + 1] = res[:, X:]
            pair = middle_rims(it, 0 if c in (0, 3) else 1)
            if c < NZC // 2:
                start_down(pair)
                zsent.append(pair)
            else:
                start_up(pair)
        for c in ZORDER:
            wait_recv(ratio_y_rims(it, c), has_ylo, has_yhi)
            for p in range(ZC * c, ZC * (c + 1), 2):
                res = y_blur([rims(rb, p), rims(rb, p + 1)], kr[1][:, :96])
                for h in range(2):
                    edge = res[:, X * h : X * (h + 1)]
                    eb[it, PAD + p + h, 0:PAD] += edge[:PAD]
                    eb[it, PAD + p + h, 2 * PAD :] += edge[PAD:]
            if c == ZORDER[2]:
                for j in range(MIDDLE, NJ):
                    pair = ratio_rims(it, j)
                    zsent.append(pair)
                    start_down(pair)
        for j in range(MIDDLE, NJ):
            start_up(ratio_rims(it, j))

        mine = v * PIECE

        def log_step(j):
            if j >= MIDDLE:
                wait_recv(ratio_rims(it, j), has_zlo, has_zhi)
            elif j == 0:
                for part in range(2):
                    wait_recv(middle_rims(it, part), has_zlo, has_zhi)
            r0, n = CHUNKS[j]
            res = z_blur(eb[it, :, r0 : r0 + n, :], kz[1])
            for g in range(n // 8):
                r = r0 + 8 * g
                logs = jnp.log(res[:, X * g : X * (g + 1)].reshape(Z, 8, X))
                for p in range(Z):
                    keep = jnp.where(own_z(own_plane(p)), own_y[r : r + 8], 0.0)
                    lg[it, p, r : r + 8, :] = keep * logs[p]
            rows = pl.ds(*CHUNKS[j])
            for i, (to, frm) in enumerate(peers):
                cp = pltpu.make_async_remote_copy(
                    src_ref=lg.at[it, pl.ds(to * PIECE, PIECE), rows],
                    dst_ref=rr.at[it, i, :, rows],
                    send_sem=rs_s.at[it, i, j], recv_sem=rs_r.at[it, i, j],
                    device_id={"view": to}, device_id_type=MESH)
                cp.start()
                vsent.append(cp)

        def sum_step(j):
            rows = pl.ds(*CHUNKS[j])
            r0, n = CHUNKS[j]
            acc = lg[it, pl.ds(mine, PIECE), r0 : r0 + n, :]
            for i in range(VIEWS - 1):
                pltpu.make_async_remote_copy(
                    src_ref=lg.at[it, pl.ds(0, PIECE), rows], dst_ref=rr.at[it, i, :, rows],
                    send_sem=rs_s.at[it, i, j], recv_sem=rs_r.at[it, i, j],
                    device_id={"view": peers[i][0]}, device_id_type=MESH).wait_recv()
                acc = acc + rr[it, i, :, r0 : r0 + n, :]
            yj = ypos[r0 : r0 + n]
            ins = [
                jnp.where((yj >= bounds_ref[2, w]) & (yj < bounds_ref[3, w]), 1.0, 0.0).astype(F32)
                for w in range(VIEWS)
            ]
            for p in range(PIECE):
                zpos = z0 + v + VIEWS * p
                count = jnp.zeros((n, X), F32)
                for w in range(VIEWS):
                    inz = (zpos >= bounds_ref[0, w]) & (zpos < bounds_ref[1, w])
                    count = count + jnp.where(inz, ins[w], 0.0)
                old = ef[it, v, p, r0 : r0 + n, :]
                new = old * jnp.exp(acc[p] / count)
                newf[it, p, r0 : r0 + n, :] = new
                if it < ITERS - 1:
                    ef[it + 1, v, p, r0 : r0 + n, :] = new
            if it < ITERS - 1:
                target = ef.at[it + 1, v, :, rows]
                send_z(owned_rims(it + 1, j))
            else:
                target = out_ref.at[0, :, v, rows]
                cp = pltpu.make_async_copy(newf.at[it, :, rows], target, lsem.at[3 + j])
                cp.start()
                vsent.append(cp)
            for i, (to, frm) in enumerate(peers):
                cp = pltpu.make_async_remote_copy(
                    src_ref=newf.at[it, :, rows], dst_ref=target,
                    send_sem=ag_s.at[it, i, j], recv_sem=ag_r.at[it, i, j],
                    device_id={"view": to}, device_id_type=MESH)
                cp.start()
                vsent.append(cp)

        def gather_step(j):
            rows = pl.ds(*CHUNKS[j])
            for i, (to, frm) in enumerate(peers):
                if it < ITERS - 1:
                    target = ef.at[it + 1, frm, :, rows]
                else:
                    target = out_ref.at[0, :, frm, rows]
                pltpu.make_async_remote_copy(
                    src_ref=newf.at[it, :, rows], dst_ref=target,
                    send_sem=ag_s.at[it, i, j], recv_sem=ag_r.at[it, i, j],
                    device_id={"view": to}, device_id_type=MESH).wait_recv()

        for n in range(NJ + S3):
            if n < NJ:
                log_step(PROC[it][n])
            if 0 <= n - S1 < NJ:
                sum_step(PROC[it][n - S1])
            if it < ITERS - 1:
                if 0 <= n - S2 < NJ:
                    j = PROC[it][n - S2]
                    wait_recv(owned_rims(it + 1, j), has_zlo, has_zhi)
                    forward(it + 1, j)
                if 0 <= n - S3 < NJ:
                    j = PROC[it][n - S3]
                    gather_step(j)
                    wait_forwards(it + 1, j)
                    blur_rows(it + 1, *CHUNKS[j])
        if it == ITERS - 1:
            for j in PROC[it]:
                gather_step(j)

    for pair in zsent:
        wait_send(pair, has_zlo, has_zhi)
    for cond, cp in ysent:

        @pl.when(cond)
        def _():
            cp.wait_send()

    for cp in vsent:
        if cp.is_remote:
            cp.wait_send()
        else:
            cp.wait()


def body(estimate, views_data, psf_taps, view_bounds):
    dma = pltpu.SemaphoreType.DMA
    return pl.pallas_call(
        kernel,
        out_shape=pltpu.VMEM((1, PIECE, VIEWS, Y, X), F32),
        in_specs=[
            pl.BlockSpec(memory_space=pltpu.SMEM),
            pl.BlockSpec(memory_space=pltpu.HBM),
            pl.BlockSpec(memory_space=pltpu.HBM),
            pl.BlockSpec(memory_space=pltpu.HBM),
        ],
        out_specs=pl.BlockSpec(memory_space=pltpu.VMEM),
        scratch_shapes=[
            pltpu.VMEM((ITERS, 16, PIECE, Y, X), F32),
            pltpu.VMEM((ITERS, Z, 80, X), F32),
            pltpu.VMEM((ITERS, Z, 80, X), F32),
            pltpu.VMEM((ITERS, 64, Y, X), F32),
            pltpu.VMEM((ITERS, Z, Y, X), F32),
            pltpu.VMEM((ITERS, VIEWS - 1, PIECE, Y, X), F32),
            pltpu.VMEM((ITERS, PIECE, Y, X), F32),
            pltpu.VMEM((Z, Y, X), F32),
            pltpu.VMEM((Z, Y, X), F32),
            pltpu.VMEM((3, 1, TAPS), F32),
            pltpu.VMEM((2, 256, 1536), BF16),
            pltpu.VMEM((2, Y, 256), BF16),
            pltpu.VMEM((2, 2 * PAD, 128), BF16),
            pltpu.VMEM((2, 256, 256), BF16),
            dma((3 + NJ + PIECE,)),
            dma((2, ITERS, NJ)),
            dma((2, ITERS, NJ)),
            dma((2, FIRST_NJ)),
            dma((2, FIRST_NJ)),
            dma((2, ITERS, 2)),
            dma((2, ITERS, 2)),
            dma((2, ITERS, NJ)),
            dma((2, ITERS, NJ)),
            dma((ITERS, VIEWS - 1, NJ)),
            dma((ITERS, VIEWS - 1, NJ)),
            dma((ITERS, 2, 2, NZC)),
            dma((ITERS, 2, 2, NZC)),
            dma((ITERS, VIEWS - 1, NJ)),
            dma((ITERS, VIEWS - 1, NJ)),
            dma((ITERS, VIEWS - 1, NJ)),
            dma((ITERS, VIEWS - 1, NJ)),
        ],
        compiler_params=pltpu.CompilerParams(
            collective_id=0, has_side_effects=True, vmem_limit_bytes=60000000
        ),
        name="deconvolve",
    )(view_bounds.T, psf_taps.transpose(1, 0, 2), estimate.reshape(1, PIECE, VIEWS, Y, X), views_data).reshape(estimate.shape)


def solution(mesh):
    return jax.shard_map(
        body,
        mesh=mesh,
        in_specs=(
            P("block", None, None, None),
            P("view", "block", None, None, None),
            P("view", None, None),
            P(),
        ),
        out_specs=P("block", None, None, None),
        check_vma=False,
    )
```

```python
import functools

import jax
import jax.numpy as jnp
from jax import lax
from jax.experimental import pallas as pl
from jax.experimental.pallas import tpu as pltpu
from jax.sharding import PartitionSpec as P

MESH = pl.DeviceIdType.MESH
F32 = jnp.float32
BF16 = jnp.bfloat16

BY = 4
ITERS = 2
Z, Y, X = 32, 48, 128
TAPS = 31
HALF = 15
PAD = 16
VIEW_X, VIEW_Y = 4, 2
VIEWS = VIEW_X * VIEW_Y
PIECE = Z // VIEWS
CHUNKS = ((16, 8), (24, 8), (0, 16), (32, 8), (40, 8))
MIDDLE = 2
PROC = ((0, 2, 3, 4, 1), (0, 1, 2, 3, 4))
NJ = len(CHUNKS)
FIRST_YC = 16
FIRST_NJ = Y // FIRST_YC
FIRST = (0, 2, 1)
S1, S2, S3 = 4, 7, 9
S1_LAST = 2
ZC = 8
NZC = Z // ZC
ZORDER = (0, 3, 1, 2)


def split(x):
    hi = x.astype(BF16)
    lo = (x - hi.astype(F32)).astype(BF16)
    return hi, lo


def fill_tap(offset, taps, flip):
    acc = jnp.zeros(offset.shape, F32)
    for k in range(TAPS):
        at = TAPS - 1 - k if flip else k
        acc = jnp.where(offset == k, taps[:, at : at + 1], acc)
    return acc


def own_plane(slot):
    return (slot >> 2) + VIEWS * (slot & 3)


def estimate_plane(slot):
    z = own_plane(slot & (Z - 1))
    return jnp.where(slot < Z, z, jnp.where((slot & 3) < 2, z + Z, z - Z))


def build_z(taps, kz_ref, f):
    def z_rows(i, _):
        r0 = pl.multiple_of(i * 16, 16)
        row = lax.broadcasted_iota(jnp.int32, (16, 512), 0) + r0
        col = lax.broadcasted_iota(jnp.int32, (16, 512), 1)
        if f == 0:
            source, target = estimate_plane(col >> 3), row >> 3
        else:
            source, target = (col >> 3) - PAD, own_plane(row >> 3)
        k = jnp.where((col & 7) == (row & 7), source - target + HALF, -1)
        hi, lo = split(fill_tap(k, taps[0], f == 1))
        kz_ref[f, pl.ds(r0, 16), 0:512] = hi
        kz_ref[f, pl.ds(r0, 16), 512:1024] = hi
        kz_ref[f, pl.ds(r0, 16), 1024:1536] = lo
        return 0

    lax.fori_loop(0, 16, z_rows, 0)


def build_xy(taps, ko_ref, kr_ref, wx_ref, f):
    row = lax.broadcasted_iota(jnp.int32, (Y, 256), 0)
    col = lax.broadcasted_iota(jnp.int32, (Y, 256), 1)
    part = jnp.where(col >= 96, 2, jnp.where(col >= 48, 1, 0))
    k = jnp.where(col < 144, col - 48 * part - row + HALF, -1)
    val = fill_tap(k, taps[1], f == 1)
    hi = val.astype(BF16).astype(F32)
    ko_ref[f] = jnp.where(part == 2, val - hi, hi).astype(BF16)

    row = lax.broadcasted_iota(jnp.int32, (2 * PAD, 128), 0)
    col = lax.broadcasted_iota(jnp.int32, (2 * PAD, 128), 1)
    part = jnp.where(col >= 64, 2, jnp.where(col >= 32, 1, 0))
    at = col - 32 * part
    source = jnp.where(at < PAD, at - PAD, at + Y - PAD)
    target = jnp.where(row < PAD, row, row + Y - 2 * PAD)
    k = jnp.where(col < 96, source - target + HALF, -1)
    val = fill_tap(k, taps[1], f == 1)
    hi = val.astype(BF16).astype(F32)
    kr_ref[f] = jnp.where(part == 2, val - hi, hi).astype(BF16)

    def x_rows(i, _):
        r0 = pl.multiple_of(i * 16, 16)
        row = lax.broadcasted_iota(jnp.int32, (16, 128), 0) + r0
        col = lax.broadcasted_iota(jnp.int32, (16, 128), 1)
        hi, lo = split(fill_tap(row - col + HALF, taps[2], f == 1))
        wx_ref[f, pl.ds(r0, 16), 0:128] = hi
        wx_ref[f, pl.ds(r0, 16), 128:256] = lo
        r1 = pl.multiple_of(r0 + 128, 16)
        wx_ref[f, pl.ds(r1, 16), 0:128] = hi
        wx_ref[f, pl.ds(r1, 16), 128:256] = jnp.zeros((16, 128), BF16)
        return 0

    lax.fori_loop(0, 8, x_rows, 0)


def z_blur(ext, kz):
    cols = [ext[:, 8 * g : 8 * g + 8, :].reshape(64 * 8, X) for g in range(ext.shape[1] // 8)]
    hi, lo = split(jnp.concatenate(cols, axis=1))
    stack = jnp.concatenate([hi, lo, hi], axis=0)
    return jnp.dot(kz, stack, preferred_element_type=F32)


def y_blur(planes, ky):
    hi, lo = split(jnp.concatenate(planes, axis=1))
    stack = jnp.concatenate([hi, lo, hi], axis=0)
    return jnp.dot(ky, stack, preferred_element_type=F32)


def x_blur(rows, wx):
    hi, lo = split(rows)
    out = jnp.dot(jnp.concatenate([hi, lo], axis=1), wx, preferred_element_type=F32)
    return out[:, :X] + out[:, X:]


def kernel(
    bounds_ref, taps_ref, est_ref, data_ref, out_ref,
    ef, ya, rb, eb, lg, rr, newf, dv, pa, taps_v, kz, ko, kr, wx,
    lsem, zs, zr, ds, dr, ms, mr, hs, hr, fs, fr, ys, yr, rs_s, rs_r, ag_s, ag_r,
):
    b = lax.axis_index("block")
    v = lax.axis_index("view")
    vx, vy = lax.rem(v, VIEW_X), lax.div(v, VIEW_X)
    bz, by = lax.div(b, BY), lax.rem(b, BY)
    n_bz = lax.axis_size("block") // BY
    has_zlo, has_zhi = bz > 0, bz < n_bz - 1
    has_ylo, has_yhi = by > 0, by < BY - 1

    peers = []
    for dy in range(VIEW_Y):
        for dx in range(VIEW_X):
            if dx or dy:
                to = lax.rem(vy + dy, VIEW_Y) * VIEW_X + lax.rem(vx + dx, VIEW_X)
                frm = lax.rem(vy + VIEW_Y - dy, VIEW_Y) * VIEW_X + lax.rem(vx + VIEW_X - dx, VIEW_X)
                peers.append((to, frm))

    load_est = [
        pltpu.make_async_copy(est_ref.at[0, m], ef.at[0, pl.ds(0, VIEWS), m], lsem.at[3 + NJ + m])
        for m in range(PIECE)
    ]
    load_data = pltpu.make_async_copy(data_ref.at[0, 0], dv, lsem.at[1])
    load_taps = pltpu.make_async_copy(taps_ref, taps_v, lsem.at[2])
    for cp in load_est:
        cp.start()
    load_data.start()
    load_taps.start()

    bar = pltpu.get_barrier_semaphore()
    total = jnp.int32(VIEWS - 1)
    for cond, dst in ((has_zlo, b - BY), (has_zhi, b + BY), (has_ylo, b - 1), (has_yhi, b + 1)):
        total = total + cond.astype(jnp.int32)

        @pl.when(cond)
        def _():
            pl.semaphore_signal(bar, inc=1, device_id={"block": dst}, device_id_type=MESH)

    for to, _ in peers:
        pl.semaphore_signal(bar, inc=1, device_id={"view": to}, device_id_type=MESH)

    for it in range(ITERS):
        eb[it, 0] = jnp.zeros((Y, X), F32)
        eb[it, 63] = jnp.zeros((Y, X), F32)

        @pl.when(jnp.logical_not(has_zlo))
        def _():
            eb[it, 1:PAD] = jnp.zeros((HALF, Y, X), F32)

        @pl.when(jnp.logical_not(has_zhi))
        def _():
            eb[it, PAD + Z : PAD + Z + HALF] = jnp.zeros((HALF, Y, X), F32)

        for cond, members in ((has_zhi, (0, 1)), (has_zlo, (3, 2))):

            @pl.when(jnp.logical_not(cond))
            def _():
                for m in members:
                    ef[it, VIEWS + v, m] = jnp.zeros((Y, X), F32)
                if it == 0:
                    for g in range(VIEWS):
                        ef[it, VIEWS + g, members[0]] = jnp.zeros((Y, X), F32)

        for buf in (ya, rb):

            @pl.when(jnp.logical_not(has_ylo))
            def _():
                buf[it, :, 0:PAD, :] = jnp.zeros((Z, PAD, X), F32)

            @pl.when(jnp.logical_not(has_yhi))
            def _():
                buf[it, :, PAD + Y :, :] = jnp.zeros((Z, PAD, X), F32)

    for cp in load_est:
        cp.wait()
    pl.semaphore_wait(bar, total)

    def z_pair(up, down, sems, recvs, key):
        out = []
        for d, (src, dst) in enumerate((up, down)):
            out.append(pltpu.make_async_remote_copy(
                src_ref=src, dst_ref=dst, send_sem=sems.at[(d,) + key], recv_sem=recvs.at[(d,) + key],
                device_id={"block": b - BY if d else b + BY}, device_id_type=MESH))
        return out

    def ratio_rims(it, j):
        rows = pl.ds(*CHUNKS[j])
        return z_pair(
            (eb.at[it, pl.ds(PAD + Z - HALF, HALF), rows], eb.at[it, pl.ds(1, HALF), rows]),
            (eb.at[it, pl.ds(PAD, HALF), rows], eb.at[it, pl.ds(PAD + Z, HALF), rows]),
            zs, zr, (it, j))

    def middle_rims(it, part):
        rows = pl.ds(16, 16)
        up = ((PAD + 24, 8, 8), (PAD + 17, 1, 7))[part]
        down = ((PAD, PAD + Z, 8), (PAD + 8, PAD + Z + 8, 7))[part]
        return z_pair(
            *((eb.at[it, pl.ds(a, k), rows], eb.at[it, pl.ds(c, k), rows]) for a, c, k in (up, down)),
            ms, mr, (it, part))

    def direct_rims(j):
        rows = pl.ds(FIRST_YC * j, FIRST_YC)
        source, target = pl.ds(0, VIEWS), pl.ds(VIEWS, VIEWS)
        return z_pair(
            (ef.at[0, source, 3, rows], ef.at[0, target, 3, rows]),
            (ef.at[0, source, 0, rows], ef.at[0, target, 0, rows]),
            ds, dr, (j,))

    def shared_rims(j):
        rows = pl.ds(FIRST_YC * j, FIRST_YC)
        return z_pair(
            (ef.at[0, v, pl.ds(2, 1), rows], ef.at[0, VIEWS + v, pl.ds(2, 1), rows]),
            (ef.at[0, v, pl.ds(1, 1), rows], ef.at[0, VIEWS + v, pl.ds(1, 1), rows]),
            hs, hr, (0, j))

    def owned_rims(it, j):
        rows = pl.ds(*CHUNKS[j])
        return z_pair(
            (newf.at[it - 1, pl.ds(2, 2), rows], ef.at[it, VIEWS + v, pl.ds(2, 2), rows]),
            (newf.at[it - 1, pl.ds(0, 2), rows], ef.at[it, VIEWS + v, pl.ds(0, 2), rows]),
            hs, hr, (it, j))

    def forwards(it, j, outgoing):
        rows = pl.ds(*CHUNKS[j]) if it else pl.ds(FIRST_YC * j, FIRST_YC)
        members = pl.ds(0, 4) if it else pl.ds(1, 2)
        out = []
        for i, (to, frm) in enumerate(peers):
            part = ef.at[it, VIEWS + (v if outgoing else frm), members, rows]
            out.append(pltpu.make_async_remote_copy(
                src_ref=part, dst_ref=part, send_sem=fs.at[it, i, j], recv_sem=fr.at[it, i, j],
                device_id={"view": to}, device_id_type=MESH))
        return out

    def forward(it, j):
        for cp in forwards(it, j, True):
            cp.start()
            vsent.append(cp)

    def wait_forwards(it, j):
        for cp in forwards(it, j, False):
            cp.wait_recv()

    def y_pair(buf, it, which, planes, n, c, half):
        up = pltpu.make_async_remote_copy(
            src_ref=buf.at[it, planes, pl.ds(Y + half, n)], dst_ref=buf.at[it, planes, pl.ds(half, n)],
            send_sem=ys.at[it, which, 0, c], recv_sem=yr.at[it, which, 0, c],
            device_id={"block": b + 1}, device_id_type=MESH)
        down = pltpu.make_async_remote_copy(
            src_ref=buf.at[it, planes, pl.ds(PAD + half, n)], dst_ref=buf.at[it, planes, pl.ds(PAD + Y + half, n)],
            send_sem=ys.at[it, which, 1, c], recv_sem=yr.at[it, which, 1, c],
            device_id={"block": b - 1}, device_id_type=MESH)
        return up, down

    def blurred_rims(it, h):
        return y_pair(ya, it, 0, pl.ds(0, Z), 8, h, 8 * h)

    def ratio_y_rims(it, c):
        return y_pair(rb, it, 1, pl.ds(ZC * c, ZC), PAD, c, 0)

    def start(pair, lo, hi):
        up, down = pair

        @pl.when(hi)
        def _():
            up.start()

        @pl.when(lo)
        def _():
            down.start()

    def wait_recv(pair, lo, hi):
        up, down = pair

        @pl.when(lo)
        def _():
            up.wait_recv()

        @pl.when(hi)
        def _():
            down.wait_recv()

    def wait_send(pair, lo, hi):
        up, down = pair

        @pl.when(hi)
        def _():
            up.wait_send()

        @pl.when(lo)
        def _():
            down.wait_send()

    zsent, ysent, vsent = [], [], []

    def send_z(pair):
        start(pair, has_zlo, has_zhi)
        zsent.append(pair)

    def send_y(up, down):
        if up is not None:

            @pl.when(has_yhi)
            def _():
                up.start()

            ysent.append((has_yhi, up))
        if down is not None:

            @pl.when(has_ylo)
            def _():
                down.start()

            ysent.append((has_ylo, down))

    def start_up(pair):
        @pl.when(has_zhi)
        def _():
            pair[0].start()

    def start_down(pair):
        @pl.when(has_zlo)
        def _():
            pair[1].start()

    for j in FIRST:
        send_z(shared_rims(j))
    for j in FIRST:
        send_z(direct_rims(j))

    load_taps.wait()
    taps = taps_v[...]
    taps = taps / jnp.sum(taps, axis=2, keepdims=True)
    build_z(taps, kz, 0)

    z0, y0 = bz * Z, by * Y
    ypos = lax.broadcasted_iota(jnp.int32, (Y, X), 0) + y0
    own_y = jnp.where((ypos >= bounds_ref[2, v]) & (ypos < bounds_ref[3, v]), 1.0, 0.0).astype(F32)

    def own_z(plane):
        zpos = z0 + plane
        return (zpos >= bounds_ref[0, v]) & (zpos < bounds_ref[1, v])

    def blur_rows(it, r0, rows):
        res = z_blur(ef[it, :, :, r0 : r0 + rows, :].reshape(64, rows, X), kz[0])
        for r in range(r0, r0 + rows, 8):
            at = X * ((r - r0) // 8)
            ya[it, :, PAD + r : PAD + r + 8, :] = res[:, at : at + X].reshape(Z, 8, X)
            if r < PAD:
                send_y(None, blurred_rims(it, r // 8)[1])
            if r >= Y - PAD:
                send_y(blurred_rims(it, (r - Y + PAD) // 8)[0], None)

    for j in FIRST:
        wait_recv(shared_rims(j), has_zlo, has_zhi)
        forward(0, j)
    build_xy(taps, ko, kr, wx, 0)
    build_xy(taps, ko, kr, wx, 1)
    build_z(taps, kz, 1)
    load_data.wait()
    for j in FIRST:
        wait_recv(direct_rims(j), has_zlo, has_zhi)
        wait_forwards(0, j)
        blur_rows(0, FIRST_YC * j, FIRST_YC)

    for it in range(ITERS):
        own = slice(PAD, PAD + Y)
        for p in range(0, Z, 2):
            res = y_blur([ya[it, p, own], ya[it, p + 1, own]], ko[0][:, :144])
            pa[p] = res[:, :X]
            pa[p + 1] = res[:, X:]
        for h in range(2):
            wait_recv(blurred_rims(it, h), has_ylo, has_yhi)

        def rims(buf, p):
            return jnp.concatenate([buf[it, p, 0:PAD], buf[it, p, PAD + Y :]], axis=0)

        for c in ZORDER:
            span = range(ZC * c, ZC * (c + 1), 2)
            parts = []
            for p in span:
                res = y_blur([rims(ya, p), rims(ya, p + 1)], kr[0][:, :96])
                for h in range(2):
                    edge = res[:, X * h : X * (h + 1)]
                    parts += [pa[p + h, 0:PAD] + edge[:PAD], pa[p + h, PAD : 2 * PAD], pa[p + h, 2 * PAD :] + edge[PAD:]]
            blurred = x_blur(jnp.concatenate(parts, axis=0), wx[0])
            ratio = dv[ZC * c : ZC * (c + 1)].reshape(ZC * Y, X) / blurred
            rb[it, ZC * c : ZC * (c + 1), own, :] = x_blur(ratio, wx[1]).reshape(ZC, Y, X)
            send_y(*ratio_y_rims(it, c))
            for p in span:
                res = y_blur([rb[it, p, own], rb[it, p + 1, own]], ko[1][:, :144])
                eb[it, PAD + p] = res[:, :X]
                eb[it, PAD + p + 1] = res[:, X:]
            pair = middle_rims(it, 0 if c in (0, 3) else 1)
            if c < NZC // 2:
                start_down(pair)
                zsent.append(pair)
            else:
                start_up(pair)
        for c in ZORDER:
            wait_recv(ratio_y_rims(it, c), has_ylo, has_yhi)
            for p in range(ZC * c, ZC * (c + 1), 2):
                res = y_blur([rims(rb, p), rims(rb, p + 1)], kr[1][:, :96])
                for h in range(2):
                    edge = res[:, X * h : X * (h + 1)]
                    eb[it, PAD + p + h, 0:PAD] += edge[:PAD]
                    eb[it, PAD + p + h, 2 * PAD :] += edge[PAD:]
            if c == ZORDER[2]:
                for j in range(MIDDLE, NJ):
                    pair = ratio_rims(it, j)
                    zsent.append(pair)
                    start_down(pair)
        for j in range(MIDDLE, NJ):
            start_up(ratio_rims(it, j))

        mine = v * PIECE

        def log_step(j):
            if j >= MIDDLE:
                wait_recv(ratio_rims(it, j), has_zlo, has_zhi)
            elif j == 0:
                for part in range(2):
                    wait_recv(middle_rims(it, part), has_zlo, has_zhi)
            r0, n = CHUNKS[j]
            res = z_blur(eb[it, :, r0 : r0 + n, :], kz[1])
            for g in range(n // 8):
                r = r0 + 8 * g
                logs = jnp.log(res[:, X * g : X * (g + 1)].reshape(Z, 8, X))
                for p in range(Z):
                    keep = jnp.where(own_z(own_plane(p)), own_y[r : r + 8], 0.0)
                    lg[it, p, r : r + 8, :] = keep * logs[p]
            rows = pl.ds(*CHUNKS[j])
            for i, (to, frm) in enumerate(peers):
                cp = pltpu.make_async_remote_copy(
                    src_ref=lg.at[it, pl.ds(to * PIECE, PIECE), rows],
                    dst_ref=rr.at[it, i, :, rows],
                    send_sem=rs_s.at[it, i, j], recv_sem=rs_r.at[it, i, j],
                    device_id={"view": to}, device_id_type=MESH)
                cp.start()
                vsent.append(cp)

        def sum_step(j):
            rows = pl.ds(*CHUNKS[j])
            r0, n = CHUNKS[j]
            acc = lg[it, pl.ds(mine, PIECE), r0 : r0 + n, :]
            for i in range(VIEWS - 1):
                pltpu.make_async_remote_copy(
                    src_ref=lg.at[it, pl.ds(0, PIECE), rows], dst_ref=rr.at[it, i, :, rows],
                    send_sem=rs_s.at[it, i, j], recv_sem=rs_r.at[it, i, j],
                    device_id={"view": peers[i][0]}, device_id_type=MESH).wait_recv()
                acc = acc + rr[it, i, :, r0 : r0 + n, :]
            yj = ypos[r0 : r0 + n]
            ins = [
                jnp.where((yj >= bounds_ref[2, w]) & (yj < bounds_ref[3, w]), 1.0, 0.0).astype(F32)
                for w in range(VIEWS)
            ]
            for p in range(PIECE):
                zpos = z0 + v + VIEWS * p
                count = jnp.zeros((n, X), F32)
                for w in range(VIEWS):
                    inz = (zpos >= bounds_ref[0, w]) & (zpos < bounds_ref[1, w])
                    count = count + jnp.where(inz, ins[w], 0.0)
                old = ef[it, v, p, r0 : r0 + n, :]
                new = old * jnp.exp(acc[p] / count)
                newf[it, p, r0 : r0 + n, :] = new
                if it < ITERS - 1:
                    ef[it + 1, v, p, r0 : r0 + n, :] = new
            if it < ITERS - 1:
                target = ef.at[it + 1, v, :, rows]
                send_z(owned_rims(it + 1, j))
            else:
                target = out_ref.at[0, :, v, rows]
                cp = pltpu.make_async_copy(newf.at[it, :, rows], target, lsem.at[3 + j])
                cp.start()
                vsent.append(cp)
            for i, (to, frm) in enumerate(peers):
                cp = pltpu.make_async_remote_copy(
                    src_ref=newf.at[it, :, rows], dst_ref=target,
                    send_sem=ag_s.at[it, i, j], recv_sem=ag_r.at[it, i, j],
                    device_id={"view": to}, device_id_type=MESH)
                cp.start()
                vsent.append(cp)

        def gather_step(j):
            rows = pl.ds(*CHUNKS[j])
            for i, (to, frm) in enumerate(peers):
                if it < ITERS - 1:
                    target = ef.at[it + 1, frm, :, rows]
                else:
                    target = out_ref.at[0, :, frm, rows]
                pltpu.make_async_remote_copy(
                    src_ref=newf.at[it, :, rows], dst_ref=target,
                    send_sem=ag_s.at[it, i, j], recv_sem=ag_r.at[it, i, j],
                    device_id={"view": to}, device_id_type=MESH).wait_recv()

        for n in range(NJ + S3):
            if n < NJ:
                log_step(PROC[it][n])
            late = S1 if it < ITERS - 1 else S1_LAST
            if 0 <= n - late < NJ:
                sum_step(PROC[it][n - late])
            if it < ITERS - 1:
                if 0 <= n - S2 < NJ:
                    j = PROC[it][n - S2]
                    wait_recv(owned_rims(it + 1, j), has_zlo, has_zhi)
                    forward(it + 1, j)
                if 0 <= n - S3 < NJ:
                    j = PROC[it][n - S3]
                    gather_step(j)
                    wait_forwards(it + 1, j)
                    blur_rows(it + 1, *CHUNKS[j])
        if it == ITERS - 1:
            for j in PROC[it]:
                gather_step(j)

    for pair in zsent:
        wait_send(pair, has_zlo, has_zhi)
    for cond, cp in ysent:

        @pl.when(cond)
        def _():
            cp.wait_send()

    for cp in vsent:
        if cp.is_remote:
            cp.wait_send()
        else:
            cp.wait()


def body(estimate, views_data, psf_taps, view_bounds):
    dma = pltpu.SemaphoreType.DMA
    return pl.pallas_call(
        kernel,
        out_shape=pltpu.VMEM((1, PIECE, VIEWS, Y, X), F32),
        in_specs=[
            pl.BlockSpec(memory_space=pltpu.SMEM),
            pl.BlockSpec(memory_space=pltpu.HBM),
            pl.BlockSpec(memory_space=pltpu.HBM),
            pl.BlockSpec(memory_space=pltpu.HBM),
        ],
        out_specs=pl.BlockSpec(memory_space=pltpu.VMEM),
        scratch_shapes=[
            pltpu.VMEM((ITERS, 16, PIECE, Y, X), F32),
            pltpu.VMEM((ITERS, Z, 80, X), F32),
            pltpu.VMEM((ITERS, Z, 80, X), F32),
            pltpu.VMEM((ITERS, 64, Y, X), F32),
            pltpu.VMEM((ITERS, Z, Y, X), F32),
            pltpu.VMEM((ITERS, VIEWS - 1, PIECE, Y, X), F32),
            pltpu.VMEM((ITERS, PIECE, Y, X), F32),
            pltpu.VMEM((Z, Y, X), F32),
            pltpu.VMEM((Z, Y, X), F32),
            pltpu.VMEM((3, 1, TAPS), F32),
            pltpu.VMEM((2, 256, 1536), BF16),
            pltpu.VMEM((2, Y, 256), BF16),
            pltpu.VMEM((2, 2 * PAD, 128), BF16),
            pltpu.VMEM((2, 256, 256), BF16),
            dma((3 + NJ + PIECE,)),
            dma((2, ITERS, NJ)),
            dma((2, ITERS, NJ)),
            dma((2, FIRST_NJ)),
            dma((2, FIRST_NJ)),
            dma((2, ITERS, 2)),
            dma((2, ITERS, 2)),
            dma((2, ITERS, NJ)),
            dma((2, ITERS, NJ)),
            dma((ITERS, VIEWS - 1, NJ)),
            dma((ITERS, VIEWS - 1, NJ)),
            dma((ITERS, 2, 2, NZC)),
            dma((ITERS, 2, 2, NZC)),
            dma((ITERS, VIEWS - 1, NJ)),
            dma((ITERS, VIEWS - 1, NJ)),
            dma((ITERS, VIEWS - 1, NJ)),
            dma((ITERS, VIEWS - 1, NJ)),
        ],
        compiler_params=pltpu.CompilerParams(
            collective_id=0, has_side_effects=True, vmem_limit_bytes=60000000
        ),
        name="deconvolve",
    )(view_bounds.T, psf_taps.transpose(1, 0, 2), estimate.reshape(1, PIECE, VIEWS, Y, X), views_data).reshape(estimate.shape)


def solution(mesh):
    return jax.shard_map(
        body,
        mesh=mesh,
        in_specs=(
            P("block", None, None, None),
            P("view", "block", None, None, None),
            P("view", None, None),
            P(),
        ),
        out_specs=P("block", None, None, None),
        check_vma=False,
    )
```
